512 devices in a mesh: expert: 8 (over z_lo, core), dp: 64 (over x, y, z_hi).
Axes of the slice: x: 4, y: 8, z: 8 (z_hi: 2, z_lo: 4; z = z_hi * 4 + z_lo), core: 2. Of those that a mesh axis runs over, the one named last changes fastest.
Arguments:
- features: bfloat16 [65536, 512], P(('expert', 'dp')), may hold values from -31 to 31
- gradients: bfloat16 [65536, 512], P(('expert', 'dp')), may hold values from -31 to 31
- route_ids: int32 [65536, 2], P(('expert', 'dp')), may hold values from 0 to 7, all different within a row; in each aligned block of 128 rows (0 to 127, 128 to 255, ...) at most 64 rows name the same one
- gate_share: float32 [65536], P(('expert', 'dp')), may hold values from 0.5 to 0.95
- token_mask: int32 [65536], P(('expert', 'dp')), may hold values 0 or 1
- damping: float32 [8, 2, 1], P('expert'), may hold values from 0.5 to 2
Outputs:
- act_inverse: float32 [8, 1, 512, 512], P(None, None, 'dp')
- grad_inverse: float32 [8, 1, 512, 512], P(None, None, 'dp')
The draws below stay inside these ranges and needn't reach their ends.
Inputs may be any that keep to these rules, and one draw needn't show every extreme that they name: `route_ids`: each token names two different experts. Among the 128 tokens of one device no expert is named by more than 64 tokens, a bound that some block reaches.
All inputs are finite; a program needn't handle non-finite values. Where the reference program divides by a largest or mean magnitude, that divisor is 1e-20 or more. No bound on the sum of `token_mask` on one device may be relied on, other than what follows from the above.
Results may differ from the reference program's by a relative error of at most 0.0003.
Values may be sent and summed in bfloat16 or wider, within the bound.
A program may use at most 64 MiB of HBM per device.

```python
import math
import jax
import jax.numpy as jnp
import numpy as np
from jax import lax

EXPERTS = 8
TOP = 2
BLOCK = 512
NBLK = 1
TOK_DEV = 128
CAP = 64
WIDTH = 512
TOKENS = 65536


def make_rows(key):
    key_normal, key_scale = jax.random.split(key, 2)
    base = jnp.clip(jax.random.normal(key_normal, (TOKENS, WIDTH), jnp.float32), -4.0, 4.0)
    column_scale = jnp.exp(jax.random.uniform(key_scale, (WIDTH,), jnp.float32, math.log(0.3), math.log(3.0)))
    mixed = (base + 0.5 * jnp.roll(base, 1, axis=1)) * column_scale[None, :]
    return mixed.astype(jnp.bfloat16)


def draw_features(key, part):
    return make_rows(jax.random.fold_in(key, 11))


def draw_gradients(key, part):
    return make_rows(jax.random.fold_in(key, 23))


def touch_ends(values, rng, smallest, high):
    shape = values.shape
    spot = [jax.random.randint(jax.random.fold_in(rng, axis), (), 0, shape[axis]) for axis in range(len(shape))]
    values = values.at[tuple(spot)].set(smallest)
    longest = shape.index(max(shape))
    spot[longest] = (spot[longest] + 1) % shape[longest]
    return values.at[tuple(spot)].set(high)


def levels(stream_key, extent, cuts, least, top_value):
    loudness = 1.0
    for position, shards_of in cuts:
        heights = jax.random.uniform(jax.random.fold_in(jax.random.fold_in(stream_key, 6), position), (shards_of,), jnp.float32, least / len(cuts), top_value / len(cuts))
        loudness = loudness * jnp.repeat(jnp.exp(heights), extent[position] // shards_of).reshape((-1,) + (1,) * (len(extent) - 1 - position))
    return loudness


def routed_block(key, own, number, rows, amount, top, reach, skew):
    sequence = jax.random.permutation(key, amount)
    crowded, ordinary = shares(amount, rows * top, reach, skew, True), shares(amount, rows * top, reach, skew, False)
    places = jnp.arange(amount)

    def named(lengths, offset_by):
        used = int((lengths > 0).sum())
        fixed = max(1, used // 4)
        passed = fixed + (places - fixed + offset_by * (used - fixed)) % max(1, amount - fixed)
        return jnp.zeros((amount,), jnp.int32).at[sequence[jnp.where(places < fixed, places, passed)]].set(jnp.asarray(lengths, jnp.int32))

    lengths = jnp.where(number % 4 == 0, named(crowded, number // 4), named(ordinary, number - number // 4 - 1))
    mixed = jax.random.permutation(jax.random.fold_in(own, 3), amount)
    donor, sink = mixed[0:amount // 2 * 2:2], mixed[1:amount // 2 * 2:2]
    slack = jnp.minimum(lengths[donor] - 1, reach - lengths[sink]) // 2
    slack = jnp.where((donor == sequence[0]) | (sink == sequence[0]) | (lengths[sink] == 0), 0, jnp.maximum(slack, 0))
    passed = jax.random.randint(jax.random.fold_in(own, 4), (amount // 2,), 0, 1 << 20) % (slack + 1)
    lengths = lengths.at[donor].add(-passed).at[sink].add(passed)
    items = jnp.searchsorted(jnp.cumsum(lengths), jnp.arange(rows * top), side="right").astype(jnp.int32)
    table = items.reshape(top, rows).T
    table = table[jax.random.permutation(jax.random.fold_in(own, 1), rows)]
    offset_by = jax.random.randint(jax.random.fold_in(own, 2), (rows, 1), 0, top)
    return jnp.take_along_axis(table, (jnp.arange(top)[None, :] + offset_by) % top, axis=1)


def shares(amount, total, most, lean, full):
    weights = [(1 << 20) // math.isqrt(grade ** lean) + 1 for grade in range(1, amount + 1)]
    largest = most if full else min(most, max(-(-total // amount), total * weights[0] // sum(weights)))
    least = 1 if total - largest >= amount - 1 else 0
    given, surplus = [largest] + [least] * (amount - 1), total - largest - least * (amount - 1)
    while surplus > 0:
        candidates = [i for i in range(1, amount) if given[i] < largest] or [i for i in range(1, amount) if given[i] < most]
        pool, budget = sum([weights[i] for i in candidates]), surplus
        for i in candidates:
            extra = min(most - given[i], max(1, budget * weights[i] // pool), surplus)
            given[i] = given[i] + extra
            surplus = surplus - extra
    return np.array(given)


def setup_inputs(seed: int = 0) -> dict:
    arg_keys = jax.random.split(jax.random.key(seed), 7)
    features = draw_features(jax.random.fold_in(arg_keys[6], 71), 0)
    gradients = draw_gradients(jax.random.fold_in(arg_keys[6], 71), 0)
    route_ids_keys = jax.random.split(jax.random.fold_in(arg_keys[2], 1), TOKENS // TOK_DEV)
    route_ids_turns = jax.random.permutation(jax.random.fold_in(arg_keys[2], 3), TOKENS // TOK_DEV)
    route_ids = jax.vmap(lambda own, number: routed_block(jax.random.fold_in(arg_keys[2], 2), own, number, TOK_DEV, EXPERTS, TOP, CAP, 2))(route_ids_keys, route_ids_turns).reshape((TOKENS, TOP))
    gate_share = jnp.clip(0.5 + 0.45 * jax.random.uniform(arg_keys[3], (TOKENS,), jnp.float32) ** levels(arg_keys[3], (TOKENS,), ((0, 512),), -0.2, 0.2), 0.5, 0.95)
    token_mask = touch_ends((jax.random.randint(arg_keys[4], (TOKENS,), 0, 8) < 7).astype(jnp.int32), jax.random.fold_in(arg_keys[4], 1), 0, 1)
    damping = jnp.clip(jnp.exp(math.log(2.0) - 1.3862944 * jax.random.uniform(arg_keys[5], (EXPERTS, 2, NBLK), jnp.float32) ** levels(arg_keys[5], (EXPERTS, 2, NBLK), ((0, 8),), -0.2, 0.2)), 0.5, 2.0)
    return dict(features=features, gradients=gradients, route_ids=route_ids, gate_share=gate_share, token_mask=token_mask, damping=damping)


def newton(iterate, matrix, whole):
    left_product = jnp.einsum("irk,ikc->irc", iterate, matrix, precision=lax.Precision.HIGHEST)
    return 2.0 * iterate - jnp.einsum("irk,ikc->irc", left_product, whole, precision=lax.Precision.HIGHEST)


def reference(features, gradients, route_ids, gate_share, token_mask, damping):
    kept_mask = token_mask.astype(jnp.float32)
    weight_pair = jnp.stack([gate_share, 1.0 - gate_share], axis=1) * kept_mask[:, None]
    rounded = (gradients.astype(jnp.float32)[:, None, :] * weight_pair[:, :, None]).astype(jnp.bfloat16)
    rounded = lax.optimization_barrier(rounded)
    pair_grads = rounded.astype(jnp.float32)
    inputs = features.astype(jnp.float32) * kept_mask[:, None]
    load_inverse = 1.0 / (TOKENS * TOP / EXPERTS)
    experts = jnp.arange(EXPERTS, dtype=jnp.int32)
    damping_flat = damping.reshape(EXPERTS, 2 * NBLK)
    identity = jnp.eye(BLOCK, dtype=jnp.float32)

    def factor_of(packed):
        expert, damping_row = packed
        chosen = (route_ids == expert).astype(jnp.float32)
        member = jnp.sum(chosen, axis=1)
        picked = jnp.sum(pair_grads * chosen[:, :, None], axis=1)
        weighted_inputs = inputs * member[:, None]
        blocks = []
        for source, weighted in ((inputs, weighted_inputs), (picked, picked)):
            for block_index in range(NBLK):
                columns = slice(block_index * BLOCK, (block_index + 1) * BLOCK)
                product = jnp.dot(weighted[:, columns].T, source[:, columns], precision=lax.Precision.HIGHEST, preferred_element_type=jnp.float32)
                blocks.append(product * load_inverse)
        gram_stack = jnp.stack(blocks)
        matrix = gram_stack + damping_row[:, None, None] * identity
        largest_sum = jnp.max(jnp.sum(jnp.abs(matrix), axis=2), axis=1)
        bound_scale = (1.0 / largest_sum)[:, None, None]
        iterate_one = 2.0 * bound_scale * identity - bound_scale * bound_scale * matrix
        iterate_two = newton(iterate_one, matrix, iterate_one)
        return newton(iterate_two, matrix, iterate_two)

    result = lax.map(factor_of, (experts, damping_flat))
    return result[:, :NBLK], result[:, NBLK:]
```

```python
import jax
import jax.numpy as jnp
from jax import lax
from jax.experimental import pallas as pl
from jax.experimental.pallas import tpu as pltpu
from jax.sharding import PartitionSpec as P

MESH = pl.DeviceIdType.MESH
BLOCK = 512
HALF = 256
TOKENS_HERE = 128
LOAD_INVERSE = 1.0 / 16384.0
F32 = jnp.float32
BF16 = jnp.bfloat16


def device_at(x, y, z, c):
    return {"expert": lax.rem(z, 4) * 2 + c, "dp": x * 16 + y * 2 + z // 4}


def split_dot(rows, high, low):
    top = rows.astype(BF16)
    rest = (rows - top.astype(F32)).astype(BF16)
    both = jnp.concatenate([top, rest], axis=0)
    first = jnp.dot(both, high, preferred_element_type=F32)
    second = jnp.dot(top, low, preferred_element_type=F32)
    count = rows.shape[0]
    return first[:count] + (first[count:] + second)


def refresh(
    feat, grad, route, share, mask, damp, out,
    tok, wts, other, other_w, spread, gram, packed, diag_out, parts, diag_parts,
    total, diag_total, high, low, rows_out,
    tok_send, tok_recv, wts_send, wts_recv, fwd_send, fwd_wsend,
    part_send, part_recv, diag_send, diag_recv, diag_back_send, diag_back_recv,
    share_send, share_recv, share_fwd, out_send, out_recv, out_fwd,
):
    expert_at, dp_at = lax.axis_index("expert"), lax.axis_index("dp")
    c, zl = lax.rem(expert_at, 2), expert_at // 2
    zh, y, x = lax.rem(dp_at, 2), lax.rem(dp_at // 2, 8), dp_at // 16
    z = zh * 4 + zl
    j, b = z // 2, lax.rem(z, 2)
    sib = 1 - c
    parity = lax.rem(x, 2)
    mate = x + 1 - 2 * parity
    cross = 3 - x
    slot_me = (y * 2 + b) * 2 + c
    source_me = y * 8 + z
    sums_diag = (y == 0) & (b == 0) & (c == 0)
    own_part = c == lax.rem(j, 2)

    def remote(src, dst, send, recv, where):
        return pltpu.make_async_remote_copy(
            src_ref=src, dst_ref=dst, send_sem=send, recv_sem=recv,
            device_id=where, device_id_type=MESH,
        )

    barrier = pltpu.get_barrier_semaphore()

    def greet(where):
        pl.semaphore_signal(barrier, inc=1, device_id=where, device_id_type=MESH)

    greet(device_at(mate, y, z, c))
    greet(device_at(cross, y, z, c))

    def greet_part(i, _):
        @pl.when(jnp.logical_not(own_part & (i == source_me)))
        def _():
            greet(device_at(x, i // 8, lax.rem(i, 8), lax.rem(j, 2)))
        return 0
    lax.fori_loop(0, 64, greet_part, 0)

    def greet_block(i, _):
        k = lax.rem(slot_me + i, 32)
        greet(device_at(x, k // 4, 2 * j + lax.rem(k // 2, 2), lax.rem(k, 2)))
        return 0
    lax.fori_loop(1, 32, greet_block, 0)

    out_self = (c == x // 2) & (b == zh) & (lax.rem(j, 2) == c)

    def greet_out(i, _):
        f, e = i // 4, 2 * lax.rem(i, 4) + c
        xs, js = 2 * f + e // 4, lax.rem(e, 4)
        @pl.when(jnp.logical_not(out_self & (xs == x) & (js == j)))
        def _():
            greet(device_at(xs, y, 2 * js + zh, x // 2))
        return 0
    lax.fori_loop(0, 8, greet_out, 0)

    lanes = lax.broadcasted_iota(jnp.int32, (8, TOKENS_HERE), 0)
    keep = jnp.broadcast_to(mask[...].astype(F32), (8, TOKENS_HERE))
    is_first = route[0:1, :] == lanes
    is_second = route[1:2, :] == lanes
    share_b = jnp.broadcast_to(share[...], (8, TOKENS_HERE))
    weight_act = jnp.where(is_first | is_second, keep, 0.0)
    weight_grad = jnp.where(is_first, share_b * keep, jnp.where(is_second, (1.0 - share_b) * keep, 0.0))

    @pl.when(x < 2)
    def _():
        tok[0] = feat[...]
        other[...] = grad[...]
        wts[0] = weight_act
        other_w[...] = weight_grad

    @pl.when(x >= 2)
    def _():
        tok[0] = grad[...]
        other[...] = feat[...]
        wts[0] = weight_grad
        other_w[...] = weight_act

    waiting = (
        2 + 64 - own_part.astype(jnp.int32) + 31 + 8 - out_self.astype(jnp.int32)
    )
    pl.semaphore_wait(barrier, waiting)

    to_cross = remote(other, tok.at[1], tok_send.at[0], tok_recv.at[1], device_at(cross, y, z, c))
    to_cross_w = remote(other_w, wts.at[1], wts_send.at[0], wts_recv.at[1], device_at(cross, y, z, c))
    to_mate = remote(tok.at[0], tok.at[2], tok_send.at[1], tok_recv.at[2], device_at(mate, y, z, c))
    to_mate_w = remote(wts.at[0], wts.at[2], wts_send.at[1], wts_recv.at[2], device_at(mate, y, z, c))
    on_mate = remote(tok.at[1], tok.at[3], tok_send.at[2], tok_recv.at[3], device_at(mate, y, z, c))
    on_mate_w = remote(wts.at[1], wts.at[3], wts_send.at[2], wts_recv.at[3], device_at(mate, y, z, c))

    def to_sib(i):
        where = device_at(x, y, z, sib)
        return (
            remote(tok.at[i], tok.at[4 + i], fwd_send.at[i], tok_recv.at[4 + i], where),
            remote(wts.at[i], wts.at[4 + i], fwd_wsend.at[i], wts_recv.at[4 + i], where),
        )

    def from_sib(i):
        for copy in to_sib(i):
            copy.wait_recv()

    def started(copies):
        for copy in copies:
            copy.start()

    def landed(copies):
        for copy in copies:
            copy.wait_recv()

    def gather_gram(i, begin):
        for kk in range(2):
            e = 4 * parity + 2 * kk + c
            for h, slot in enumerate((i, 4 + i)):
                row = wts[slot, pl.ds(e, 1), :]
                column = jnp.transpose(jnp.broadcast_to(row, (TOKENS_HERE, TOKENS_HERE)))
                for q in range(4):
                    piece = tok[slot, :, 128 * q : 128 * q + 128].astype(F32) * column
                    spread[kk, 128 * h : 128 * h + 128, 128 * q : 128 * q + 128] = piece.astype(BF16)
            left, right = spread[kk, :, :HALF], spread[kk, :, HALF:]
            for n, (one, two) in enumerate(((left, right), (left, left), (right, right))):
                term = lax.dot_general(one, two, (((0,), (0,)), ((), ())), preferred_element_type=F32)
                gram[kk, n] = term if begin else gram[kk, n] + term

    started((to_cross_w, to_cross, to_mate_w, to_mate))
    started(to_sib(0))
    from_sib(0)
    gather_gram(0, True)
    landed((to_cross_w, to_cross))
    started((on_mate_w, on_mate))
    started(to_sib(1))
    landed((to_mate_w, to_mate))
    started(to_sib(2))
    from_sib(1)
    gather_gram(1, False)
    landed((on_mate_w, on_mate))
    started(to_sib(3))
    from_sib(2)
    gather_gram(2, False)
    from_sib(3)
    gather_gram(3, False)

    r_half = lax.broadcasted_iota(jnp.int32, (HALF, HALF), 0)
    c_half = lax.broadcasted_iota(jnp.int32, (HALF, HALF), 1)
    damp_row = jnp.where(x < 2, damp[0:1, :], damp[1:2, :])
    for kk in range(2):
        upper, lower = gram[kk, 1], gram[kk, 2]
        packed[kk, 0:16] = gram[kk, 0].astype(BF16).reshape(16, 16, HALF)
        packed[kk, 16:32] = jnp.where(r_half <= c_half, upper, lower).astype(BF16).reshape(16, 16, HALF)
        on_diag = r_half == c_half
        d_up = jnp.sum(jnp.where(on_diag, upper, 0.0), axis=0, keepdims=True)
        d_low = jnp.sum(jnp.where(on_diag, lower, 0.0), axis=0, keepdims=True)
        mine = (expert_at == 4 * parity + 2 * kk + c) & (y == 0) & (zh == 0)
        diag_out[kk, 0:1] = d_up[:, :128]
        diag_out[kk, 1:2] = d_up[:, 128:]
        diag_out[kk, 2:3] = d_low[:, :128]
        diag_out[kk, 3:4] = d_low[:, 128:]
        diag_out[kk, 4:8] = jnp.broadcast_to(jnp.where(mine, damp_row, 0.0), (4, 128))

    def part_copy(kk, k):
        jj = 2 * kk + c
        where = device_at(x, k // 4, 2 * jj + lax.rem(k // 2, 2), lax.rem(k, 2))
        return remote(packed.at[kk, k], parts.at[source_me], part_send.at[kk, k], part_recv, where)

    def is_me(kk, k):
        return own_part & (2 * kk + c == j) & (k == slot_me)

    for kk in range(2):
        jj = 2 * kk + c
        there = (y == 0) & (c == 0) & (z == 2 * jj)
        diag_copy = remote(
            diag_out.at[kk], diag_parts.at[source_me], diag_send.at[kk], diag_recv,
            device_at(x, 0, 2 * jj, 0),
        )

        @pl.when(jnp.logical_not(there))
        def _():
            diag_copy.start()

        @pl.when(there)
        def _():
            pltpu.make_async_copy(diag_out.at[kk], diag_parts.at[source_me], diag_recv).start()

        def send_part(i, _):
            k = lax.rem(slot_me + i, 32)

            @pl.when(jnp.logical_not(is_me(kk, k)))
            def _():
                part_copy(kk, k).start()

            @pl.when(is_me(kk, k))
            def _():
                pltpu.make_async_copy(packed.at[kk, k], parts.at[source_me], part_recv).start()
            return 0
        lax.fori_loop(0, 32, send_part, 0)

    pltpu.make_async_copy(parts, parts, part_recv).wait()
    summed = parts[0].astype(F32)
    for i in range(1, 64):
        summed = summed + parts[i].astype(F32)
    total[slot_me] = summed

    def share_copy(i):
        k = lax.rem(slot_me + 2 * i, 32)
        where = device_at(x, k // 4, 2 * j + lax.rem(k // 2, 2), c)
        return remote(total.at[slot_me], total.at[slot_me], share_send.at[i], share_recv.at[slot_me], where)

    def share_on(k):
        return remote(
            total.at[k], total.at[k], share_fwd.at[k // 2], share_recv.at[k], device_at(x, y, z, sib)
        )

    def send_share(i, _):
        share_copy(i).start()
        return 0
    lax.fori_loop(1, 16, send_share, 0)
    share_on(slot_me).start()

    def diag_back(k):
        where = device_at(x, k // 4, 2 * j + lax.rem(k // 2, 2), lax.rem(k, 2))
        return remote(diag_total, diag_total, diag_back_send.at[k], diag_back_recv, where)

    @pl.when(sums_diag)
    def _():
        pltpu.make_async_copy(diag_parts, diag_parts, diag_recv).wait()
        diag_total[...] = jnp.sum(diag_parts[...], axis=0)

        def send_diag(k, _):
            diag_back(k).start()
            return 0
        lax.fori_loop(1, 32, send_diag, 0)

    def pass_on(i, _):
        k = lax.rem(slot_me + 32 - 2 * i, 32)
        share_on(k).wait_recv()
        share_on(k).start()
        return 0
    lax.fori_loop(1, 16, pass_on, 0)

    def from_other(i, _):
        share_on(2 * i + sib).wait_recv()
        return 0
    lax.fori_loop(0, 16, from_other, 0)

    @pl.when(jnp.logical_not(sums_diag))
    def _():
        diag_back(0).wait_recv()

    corner = total[0:16].reshape(HALF, HALF) * LOAD_INVERSE
    folded = total[16:32].reshape(HALF, HALF) * LOAD_INVERSE
    turned = jnp.transpose(folded)
    damping = diag_total[4:5, :]
    d_up = jnp.concatenate(
        [diag_total[0:1] * LOAD_INVERSE + damping, diag_total[1:2] * LOAD_INVERSE + damping], axis=1
    )
    d_low = jnp.concatenate(
        [diag_total[2:3] * LOAD_INVERSE + damping, diag_total[3:4] * LOAD_INVERSE + damping], axis=1
    )
    upper = jnp.where(r_half < c_half, folded, jnp.where(r_half > c_half, turned, d_up))
    lower = jnp.where(r_half > c_half, folded, jnp.where(r_half < c_half, turned, d_low))
    corner_turned = jnp.transpose(corner)
    sums_left = jnp.sum(jnp.abs(upper) + jnp.abs(corner_turned), axis=0, keepdims=True)
    sums_right = jnp.sum(jnp.abs(corner) + jnp.abs(lower), axis=0, keepdims=True)
    largest = jnp.max(jnp.maximum(sums_left, sums_right), axis=1, keepdims=True)
    scale = 1.0 / largest
    one = jnp.where(r_half == c_half, 1.0, 0.0)
    for block, at in (
        (one - scale * upper, (slice(0, HALF), slice(0, HALF))),
        (-scale * corner, (slice(0, HALF), slice(HALF, BLOCK))),
        (-scale * corner_turned, (slice(HALF, BLOCK), slice(0, HALF))),
        (one - scale * lower, (slice(HALF, BLOCK), slice(HALF, BLOCK))),
    ):
        top = block.astype(BF16)
        high[at] = top
        low[at] = (block - top.astype(F32)).astype(BF16)

    row_at = lax.broadcasted_iota(jnp.int32, (16, BLOCK), 0)
    col_at = lax.broadcasted_iota(jnp.int32, (16, BLOCK), 1)
    wanted = 8 * (16 * (2 * c + row_at // 8) + 2 * y + b) + lax.rem(row_at, 8)
    unit = jnp.where(col_at == wanted, 1.0, 0.0)
    lead = unit
    for _ in range(7):
        lead = unit + split_dot(lead, high[...], low[...])
    result = lead * scale
    rows_out[0] = result[:8]
    rows_out[1] = result[8:]

    f_me, e_me = x // 2, 4 * parity + j
    core_there = lax.rem(j, 2)

    def out_copy(n):
        i, zt = n // 4, 4 * b + lax.rem(n, 4)
        return remote(
            rows_out.at[i], out.at[f_me, e_me], out_send.at[n], out_recv.at[f_me * 8 + e_me],
            device_at(2 * c + i, y, zt, core_there),
        )

    def out_here(n):
        return (2 * c + n // 4 == x) & (4 * b + lax.rem(n, 4) == z) & (core_there == c)

    def send_out(n, _):
        @pl.when(jnp.logical_not(out_here(n)))
        def _():
            out_copy(n).start()

        @pl.when(out_here(n))
        def _():
            pltpu.make_async_copy(
                rows_out.at[n // 4], out.at[f_me, e_me], out_recv.at[f_me * 8 + e_me]
            ).start()
        return 0
    lax.fori_loop(0, 8, send_out, 0)

    def out_on(f, e):
        return remote(
            out.at[f, e], out.at[f, e], out_fwd.at[f * 4 + e // 2], out_recv.at[f * 8 + e],
            device_at(x, y, z, sib),
        )

    def pass_out(n, _):
        copy = out_on(n // 4, 2 * lax.rem(n, 4) + c)
        copy.wait_recv()
        copy.start()
        return 0
    lax.fori_loop(0, 8, pass_out, 0)

    def take_out(n, _):
        out_on(n // 4, 2 * lax.rem(n, 4) + sib).wait_recv()
        return 0
    lax.fori_loop(0, 8, take_out, 0)

    for copy in (to_cross, to_cross_w, to_mate, to_mate_w, on_mate, on_mate_w):
        copy.wait_send()
    for i in range(4):
        for copy in to_sib(i):
            copy.wait_send()
    for kk in range(2):
        jj = 2 * kk + c

        @pl.when(jnp.logical_not((y == 0) & (c == 0) & (z == 2 * jj)))
        def _():
            remote(
                diag_out.at[kk], diag_parts.at[source_me], diag_send.at[kk], diag_recv,
                device_at(x, 0, 2 * jj, 0),
            ).wait_send()

        def part_left(k, _):
            @pl.when(jnp.logical_not(is_me(kk, k)))
            def _():
                part_copy(kk, k).wait_send()
            return 0
        lax.fori_loop(0, 32, part_left, 0)

    def share_left(i, _):
        share_copy(i).wait_send()
        return 0
    lax.fori_loop(1, 16, share_left, 0)

    def share_on_left(i, _):
        share_on(2 * i + c).wait_send()
        return 0
    lax.fori_loop(0, 16, share_on_left, 0)

    @pl.when(sums_diag)
    def _():
        def diag_left(k, _):
            diag_back(k).wait_send()
            return 0
        lax.fori_loop(1, 32, diag_left, 0)

    def out_left(n, _):
        @pl.when(jnp.logical_not(out_here(n)))
        def _():
            out_copy(n).wait_send()
        return 0
    lax.fori_loop(0, 8, out_left, 0)

    def out_on_left(n, _):
        out_on(n // 4, 2 * lax.rem(n, 4) + c).wait_send()
        return 0
    lax.fori_loop(0, 8, out_on_left, 0)


def on_device(features, gradients, route_ids, gate_share, token_mask, damping):
    route = route_ids.T
    share = gate_share.reshape(1, TOKENS_HERE)
    mask = token_mask.reshape(1, TOKENS_HERE)
    damp = jnp.broadcast_to(damping.reshape(2, 1), (2, 128))
    dma = pltpu.SemaphoreType.DMA
    out = pl.pallas_call(
        refresh,
        out_shape=jax.ShapeDtypeStruct((2, 8, 8, BLOCK), F32),
        in_specs=[pl.BlockSpec(memory_space=pltpu.VMEM)] * 6,
        out_specs=pl.BlockSpec(memory_space=pltpu.VMEM),
        scratch_shapes=[
            pltpu.VMEM((8, TOKENS_HERE, BLOCK), BF16),
            pltpu.VMEM((8, 8, TOKENS_HERE), F32),
            pltpu.VMEM((TOKENS_HERE, BLOCK), BF16),
            pltpu.VMEM((8, TOKENS_HERE), F32),
            pltpu.VMEM((2, 2 * TOKENS_HERE, BLOCK), BF16),
            pltpu.VMEM((2, 3, HALF, HALF), F32),
            pltpu.VMEM((2, 32, 16, HALF), BF16),
            pltpu.VMEM((2, 8, 128), F32),
            pltpu.VMEM((64, 16, HALF), BF16),
            pltpu.VMEM((64, 8, 128), F32),
            pltpu.VMEM((32, 16, HALF), F32),
            pltpu.VMEM((8, 128), F32),
            pltpu.VMEM((BLOCK, BLOCK), BF16),
            pltpu.VMEM((BLOCK, BLOCK), BF16),
            pltpu.VMEM((2, 8, BLOCK), F32),
            dma((3,)), dma((8,)), dma((3,)), dma((8,)), dma((4,)), dma((4,)),
            dma((2, 32)), dma, dma((2,)), dma, dma((32,)), dma,
            dma((16,)), dma((32,)), dma((16,)), dma((8,)), dma((16,)), dma((8,)),
        ],
        compiler_params=pltpu.CompilerParams(
            collective_id=0, has_side_effects=True, vmem_limit_bytes=40 * 1024 * 1024
        ),
    )(features, gradients, route, share, mask, damp)
    return out[0].reshape(8, 1, 8, BLOCK), out[1].reshape(8, 1, 8, BLOCK)


def solution(mesh):
    placed = (
        P(("expert", "dp"), None),
        P(("expert", "dp"), None),
        P(("expert", "dp"), None),
        P(("expert", "dp")),
        P(("expert", "dp")),
        P("expert", None, None),
    )
    return jax.shard_map(
        on_device,
        mesh=mesh,
        in_specs=placed,
        out_specs=(P(None, None, "dp", None), P(None, None, "dp", None)),
        check_vma=False,
    )
```

```python
import jax
import jax.numpy as jnp
from jax import lax
from jax.experimental import pallas as pl
from jax.experimental.pallas import tpu as pltpu
from jax.sharding import PartitionSpec as P

MESH = pl.DeviceIdType.MESH
BLOCK = 512
HALF = 256
TOKENS_HERE = 128
LOAD_INVERSE = 1.0 / 16384.0
F32 = jnp.float32
BF16 = jnp.bfloat16


def device_at(x, y, z, c):
    return {"expert": lax.rem(z, 4) * 2 + c, "dp": x * 16 + y * 2 + lax.div(z, 4)}


def split_dot(rows, high, low):
    top = rows.astype(BF16)
    rest = (rows - top.astype(F32)).astype(BF16)
    both = jnp.concatenate([top, rest], axis=0)
    first = jnp.dot(both, high, preferred_element_type=F32)
    second = jnp.dot(top, low, preferred_element_type=F32)
    count = rows.shape[0]
    return first[:count] + (first[count:] + second)


def refresh(
    feat, grad, route_in, share_in, mask_in, damp_in, out,
    route, share, mask, damp,
    tok, wts, other, other_w, spread, gram, corners, folds, diag_out,
    by_z, by_y, z_sums, y_sums, last, diag_parts,
    total, diag_total, high, low, rows_out,
    load_sem, tok_send, tok_recv, wts_send, wts_recv, fwd_send, fwd_wsend, both_in,
    z_send, z_recv, y_send, y_recv, z2_send, y2_send, last_recv,
    diag_send, diag_recv, diag_back_send, diag_back_recv,
    share_send, share_recv, share_fwd, out_send, out_recv, out_fwd,
):
    expert_at, dp_at = lax.axis_index("expert"), lax.axis_index("dp")
    c, zl = lax.rem(expert_at, 2), lax.div(expert_at, 2)
    zh, y, x = lax.rem(dp_at, 2), lax.rem(lax.div(dp_at, 2), 8), lax.div(dp_at, 16)
    z = zh * 4 + zl
    j, b = lax.div(z, 2), lax.rem(z, 2)
    sib = 1 - c
    parity, half_x = lax.rem(x, 2), lax.div(x, 2)
    mate = x + 1 - 2 * parity
    cross = 3 - x
    row_me = jnp.where(c == 0, b * 8 + y, y * 2 + b)
    chip_me = y * 2 + b
    sums_diag = (y == 0) & (b == 0) & (c == 0)
    sums_z = c == lax.rem(j, 2)
    sibling = {"expert": expert_at + 1 - 2 * c, "dp": dp_at}

    def remote(src, dst, send, recv, where):
        return pltpu.make_async_remote_copy(
            src_ref=src, dst_ref=dst, send_sem=send, recv_sem=recv,
            device_id=where, device_id_type=MESH,
        )

    loads = (
        (route_in, route), (share_in, share), (mask_in, mask), (damp_in, damp),
    )
    for n, (src, dst) in enumerate(loads):
        pltpu.make_async_copy(src, dst, load_sem.at[n]).start()

    @pl.when(x < 2)
    def _():
        pltpu.make_async_copy(feat, tok.at[0], load_sem.at[4]).start()
        pltpu.make_async_copy(grad, other, load_sem.at[5]).start()

    @pl.when(x >= 2)
    def _():
        pltpu.make_async_copy(grad, tok.at[0], load_sem.at[4]).start()
        pltpu.make_async_copy(feat, other, load_sem.at[5]).start()

    barrier = pltpu.get_barrier_semaphore()

    def greet(where):
        pl.semaphore_signal(barrier, inc=1, device_id=where, device_id_type=MESH)

    greet(device_at(mate, y, z, c))
    greet(device_at(cross, y, z, c))
    greet(sibling)
    for n in range(1, 8):
        greet({"expert": expert_at, "dp": x * 16 + lax.rem(y + n, 8) * 2 + zh})
        greet(device_at(x, y, lax.rem(z + n, 8), c))

    for n, (src, dst) in enumerate(loads):
        pltpu.make_async_copy(src, dst, load_sem.at[n]).wait()
    lanes = lax.broadcasted_iota(jnp.int32, (8, TOKENS_HERE), 0)
    keep = jnp.broadcast_to(mask[...].astype(F32), (8, TOKENS_HERE))
    is_first = route[0:1, :] == lanes
    is_second = route[1:2, :] == lanes
    share_b = jnp.broadcast_to(share[...], (8, TOKENS_HERE))
    weight_act = jnp.where(is_first | is_second, keep, 0.0)
    weight_grad = jnp.where(is_first, share_b * keep, jnp.where(is_second, (1.0 - share_b) * keep, 0.0))

    @pl.when(x < 2)
    def _():
        wts[0] = weight_act
        other_w[...] = weight_grad

    @pl.when(x >= 2)
    def _():
        wts[0] = weight_grad
        other_w[...] = weight_act

    pltpu.make_async_copy(feat, tok.at[0], load_sem.at[4]).wait()
    pltpu.make_async_copy(grad, other, load_sem.at[5]).wait()
    pl.semaphore_wait(barrier, 17)
    pl.semaphore_signal(both_in, inc=1, device_id=sibling, device_id_type=MESH)

    to_cross = remote(other, tok.at[1], tok_send.at[0], tok_recv.at[1], device_at(cross, y, z, c))
    to_cross_w = remote(other_w, wts.at[1], wts_send.at[0], wts_recv.at[1], device_at(cross, y, z, c))
    to_mate = remote(tok.at[0], tok.at[2], tok_send.at[1], tok_recv.at[2], device_at(mate, y, z, c))
    to_mate_w = remote(wts.at[0], wts.at[2], wts_send.at[1], wts_recv.at[2], device_at(mate, y, z, c))
    on_mate = remote(tok.at[1], tok.at[3], tok_send.at[2], tok_recv.at[3], device_at(mate, y, z, c))
    on_mate_w = remote(wts.at[1], wts.at[3], wts_send.at[2], wts_recv.at[3], device_at(mate, y, z, c))

    def to_sib(i):
        where = sibling
        return (
            remote(tok.at[i], tok.at[4 + i], fwd_send.at[i], tok_recv.at[4 + i], where),
            remote(wts.at[i], wts.at[4 + i], fwd_wsend.at[i], wts_recv.at[4 + i], where),
        )

    def from_sib(i):
        for copy in to_sib(i):
            copy.wait_recv()

    def started(copies):
        for copy in copies:
            copy.start()

    def landed(copies):
        for copy in copies:
            copy.wait_recv()

    def gather_gram(i, begin):
        for kk in range(2):
            e = 4 * parity + 2 * kk + c
            for h, slot in enumerate((i, 4 + i)):
                row = wts[slot, pl.ds(e, 1), :]
                column = jnp.transpose(jnp.broadcast_to(row, (TOKENS_HERE, TOKENS_HERE)))
                for q in range(4):
                    piece = tok[slot, :, 128 * q : 128 * q + 128].astype(F32) * column
                    spread[kk, 128 * h : 128 * h + 128, 128 * q : 128 * q + 128] = piece.astype(BF16)
            left, right = spread[kk, :, :HALF], spread[kk, :, HALF:]
            for n, (one, two) in enumerate(((left, right), (left, left), (right, right))):
                term = lax.dot_general(one, two, (((0,), (0,)), ((), ())), preferred_element_type=F32)
                gram[kk, n] = term if begin else gram[kk, n] + term

    started((to_cross_w, to_cross, to_mate_w, to_mate))
    started(to_sib(0))
    from_sib(0)
    gather_gram(0, True)
    landed((to_cross_w, to_cross))
    started((on_mate_w, on_mate))
    started(to_sib(1))
    landed((to_mate_w, to_mate))
    started(to_sib(2))
    from_sib(1)
    gather_gram(1, False)
    landed((on_mate_w, on_mate))
    started(to_sib(3))
    from_sib(2)
    gather_gram(2, False)
    from_sib(3)
    gather_gram(3, False)

    pl.semaphore_wait(both_in, 1)

    def z_copy(kk, bb):
        return remote(
            corners.at[kk, pl.ds(8 * bb, 8)], by_z.at[z], z_send.at[kk, bb], z_recv.at[z],
            device_at(x, y, 4 * kk + 2 * c + bb, c),
        )

    def z_self(kk, bb):
        return z == 4 * kk + 2 * c + bb

    def y_copy(n):
        there = lax.rem(y + n, 8)
        return remote(
            folds.at[there], by_y.at[y], y_send.at[n], y_recv.at[y],
            {"expert": expert_at, "dp": x * 16 + there * 2 + zh},
        )

    def own_z():
        return pltpu.make_async_copy(corners.at[lax.div(z, 4), pl.ds(8 * b, 8)], by_z.at[z], z_recv.at[z])

    def own_y():
        return pltpu.make_async_copy(folds.at[y], by_y.at[y], y_recv.at[y])

    r_half = lax.broadcasted_iota(jnp.int32, (HALF, HALF), 0)
    c_half = lax.broadcasted_iota(jnp.int32, (HALF, HALF), 1)
    on_diag = r_half == c_half
    for kk in range(2):
        corners[kk] = gram[kk, 0].astype(BF16).reshape(16, 16, HALF)
        for bb in range(2):
            @pl.when(jnp.logical_not(z_self(kk, bb)))
            def _():
                z_copy(kk, bb).start()
    for kk in range(2):
        upper, lower = gram[kk, 1], gram[kk, 2]
        folded = jnp.where(r_half <= c_half, upper, lower).astype(BF16)
        folds[:, kk] = folded.reshape(8, 2, 16, HALF)
    for n in range(1, 8):
        y_copy(n).start()
    own_y().start()

    @pl.when(sums_z)
    def _():
        own_z().start()

    damp_row = jnp.where(x < 2, damp[0:1, :], damp[1:2, :])
    for kk in range(2):
        upper, lower = gram[kk, 1], gram[kk, 2]
        d_up = jnp.sum(jnp.where(on_diag, upper, 0.0), axis=0, keepdims=True)
        d_low = jnp.sum(jnp.where(on_diag, lower, 0.0), axis=0, keepdims=True)
        mine = (expert_at == 4 * parity + 2 * kk + c) & (y == 0) & (zh == 0)
        diag_out[kk, 0:1] = d_up[:, :128]
        diag_out[kk, 1:2] = d_up[:, 128:]
        diag_out[kk, 2:3] = d_low[:, :128]
        diag_out[kk, 3:4] = d_low[:, 128:]
        diag_out[kk, 4:8] = jnp.broadcast_to(jnp.where(mine, damp_row, 0.0), (4, 128))

    sum_y = None
    for n in range(8):
        there = lax.rem(y + 8 - n, 8)
        pltpu.make_async_copy(folds.at[0], by_y.at[there], y_recv.at[there]).wait()
        term = by_y[there].astype(F32)
        sum_y = term if n == 0 else sum_y + term
    y_sums[...] = sum_y

    def y2_copy(kk, bb):
        return remote(
            y_sums.at[kk, bb], last.at[z], y2_send.at[kk, bb], last_recv.at[z],
            device_at(x, y, 4 * kk + 2 * c + bb, 1),
        )

    def y2_self(kk, bb):
        return (c == 1) & z_self(kk, bb)

    for kk in range(2):
        for bb in range(2):
            @pl.when(jnp.logical_not(y2_self(kk, bb)))
            def _():
                y2_copy(kk, bb).start()

            @pl.when(y2_self(kk, bb))
            def _():
                pltpu.make_async_copy(y_sums.at[kk, bb], last.at[z], last_recv.at[z]).start()

    def diag_copy(kk):
        return remote(
            diag_out.at[kk], diag_parts.at[y * 8 + z], diag_send.at[kk], diag_recv,
            device_at(x, 0, 4 * kk + 2 * c, 0),
        )

    def diag_self(kk):
        return (y == 0) & (c == 0) & (z == 4 * kk)

    for kk in range(2):
        @pl.when(jnp.logical_not(diag_self(kk)))
        def _():
            diag_copy(kk).start()

        @pl.when(diag_self(kk))
        def _():
            pltpu.make_async_copy(diag_out.at[kk], diag_parts.at[y * 8 + z], diag_recv).start()

    def z2_copy(there):
        return remote(
            z_sums.at[there], last.at[y], z2_send.at[there], last_recv.at[y],
            device_at(x, there, z, 0),
        )

    def z2_self(there):
        return (c == 0) & (there == y)

    @pl.when(sums_z)
    def _():
        sum_z = None
        for n in range(8):
            there = lax.rem(z + 8 - n, 8)
            pltpu.make_async_copy(by_z.at[there], by_z.at[there], z_recv.at[there]).wait()
            term = by_z[there].astype(F32)
            sum_z = term if n == 0 else sum_z + term
        z_sums[...] = sum_z

        def z2_start(n, _):
            there = lax.rem(y + n, 8)

            @pl.when(jnp.logical_not(z2_self(there)))
            def _():
                z2_copy(there).start()

            @pl.when(z2_self(there))
            def _():
                pltpu.make_async_copy(z_sums.at[there], last.at[y], last_recv.at[y]).start()
            return 0
        lax.fori_loop(0, 8, z2_start, 0)

    summed = None
    for n in range(8):
        pltpu.make_async_copy(last.at[n], last.at[n], last_recv.at[n]).wait()
        summed = last[n] if n == 0 else summed + last[n]
    total[c, row_me] = summed

    def row_of(core, chip):
        yy, bb = lax.div(chip, 2), lax.rem(chip, 2)
        return jnp.where(core == 0, bb * 8 + yy, yy * 2 + bb)

    def share_copy(i):
        k = lax.rem(chip_me + i, 16)
        where = device_at(x, lax.div(k, 2), 2 * j + lax.rem(k, 2), c)
        own = total.at[c, row_me]
        return remote(own, own, share_send.at[i], share_recv.at[c, row_me], where)

    def share_on(row):
        one = total.at[c, row]
        return remote(one, one, share_fwd.at[row], share_recv.at[c, row], sibling)

    def send_share(i, _):
        share_copy(i).start()
        return 0
    lax.fori_loop(1, 16, send_share, 0)
    share_on(row_me).start()

    def diag_back(k):
        where = device_at(x, lax.div(k, 4), 2 * j + lax.rem(lax.div(k, 2), 2), lax.rem(k, 2))
        return remote(diag_total, diag_total, diag_back_send.at[k], diag_back_recv, where)

    @pl.when(sums_diag)
    def _():
        pltpu.make_async_copy(diag_parts, diag_parts, diag_recv).wait()
        diag_total[...] = jnp.sum(diag_parts[...], axis=0)

        def send_diag(k, _):
            diag_back(k).start()
            return 0
        lax.fori_loop(1, 32, send_diag, 0)

    def pass_on(i, _):
        row = row_of(c, lax.rem(chip_me + 16 - i, 16))
        share_on(row).wait_recv()
        share_on(row).start()
        return 0
    lax.fori_loop(1, 16, pass_on, 0)

    def from_other(row, _):
        one = total.at[sib, row]
        remote(one, one, share_fwd.at[row], share_recv.at[sib, row], sibling).wait_recv()
        return 0
    lax.fori_loop(0, 16, from_other, 0)

    @pl.when(jnp.logical_not(sums_diag))
    def _():
        diag_back(0).wait_recv()

    corner = total[0].reshape(HALF, HALF) * LOAD_INVERSE
    folded = total[1].reshape(HALF, HALF) * LOAD_INVERSE
    turned = jnp.transpose(folded)
    damping = diag_total[4:5, :]
    d_up = jnp.concatenate(
        [diag_total[0:1] * LOAD_INVERSE + damping, diag_total[1:2] * LOAD_INVERSE + damping], axis=1
    )
    d_low = jnp.concatenate(
        [diag_total[2:3] * LOAD_INVERSE + damping, diag_total[3:4] * LOAD_INVERSE + damping], axis=1
    )
    upper = jnp.where(r_half < c_half, folded, jnp.where(r_half > c_half, turned, d_up))
    lower = jnp.where(r_half > c_half, folded, jnp.where(r_half < c_half, turned, d_low))
    corner_turned = jnp.transpose(corner)
    sums_left = jnp.sum(jnp.abs(upper) + jnp.abs(corner_turned), axis=0, keepdims=True)
    sums_right = jnp.sum(jnp.abs(corner) + jnp.abs(lower), axis=0, keepdims=True)
    largest = jnp.max(jnp.maximum(sums_left, sums_right), axis=1, keepdims=True)
    scale = 1.0 / largest
    one = jnp.where(r_half == c_half, 1.0, 0.0)
    for block, at in (
        (one - scale * upper, (slice(0, HALF), slice(0, HALF))),
        (-scale * corner, (slice(0, HALF), slice(HALF, BLOCK))),
        (-scale * corner_turned, (slice(HALF, BLOCK), slice(0, HALF))),
        (one - scale * lower, (slice(HALF, BLOCK), slice(HALF, BLOCK))),
    ):
        top = block.astype(BF16)
        high[at] = top
        low[at] = (block - top.astype(F32)).astype(BF16)

    row_at = lax.broadcasted_iota(jnp.int32, (16, BLOCK), 0)
    col_at = lax.broadcasted_iota(jnp.int32, (16, BLOCK), 1)
    wanted = 8 * (16 * (2 * c + lax.div(row_at, 8)) + 2 * y + b) + lax.rem(row_at, 8)
    unit = jnp.where(col_at == wanted, 1.0, 0.0)
    lead = unit
    for _ in range(7):
        lead = unit + split_dot(lead, high[...], low[...])
    result = lead * scale
    rows_out[0] = result[:8]
    rows_out[1] = result[8:]

    f_me, e_me = half_x, 4 * parity + j
    core_there = lax.rem(j, 2)

    def out_copy(n):
        i, zt = lax.div(n, 4), 4 * b + lax.rem(n, 4)
        return remote(
            rows_out.at[i], out.at[f_me, e_me], out_send.at[n], out_recv.at[f_me * 8 + e_me],
            device_at(2 * c + i, y, zt, core_there),
        )

    def out_here(n):
        return (2 * c + lax.div(n, 4) == x) & (4 * b + lax.rem(n, 4) == z) & (core_there == c)

    def send_out(n, _):
        @pl.when(jnp.logical_not(out_here(n)))
        def _():
            out_copy(n).start()

        @pl.when(out_here(n))
        def _():
            pltpu.make_async_copy(
                rows_out.at[lax.div(n, 4)], out.at[f_me, e_me], out_recv.at[f_me * 8 + e_me]
            ).start()
        return 0
    lax.fori_loop(0, 8, send_out, 0)

    def out_on(f, e):
        return remote(
            out.at[f, e], out.at[f, e], out_fwd.at[f * 4 + lax.div(e, 2)], out_recv.at[f * 8 + e],
            sibling,
        )

    def pass_out(n, _):
        copy = out_on(lax.div(n, 4), 2 * lax.rem(n, 4) + c)
        copy.wait_recv()
        copy.start()
        return 0
    lax.fori_loop(0, 8, pass_out, 0)

    def take_out(n, _):
        out_on(lax.div(n, 4), 2 * lax.rem(n, 4) + sib).wait_recv()
        return 0
    lax.fori_loop(0, 8, take_out, 0)

    for copy in (to_cross, to_cross_w, to_mate, to_mate_w, on_mate, on_mate_w):
        copy.wait_send()
    for i in range(4):
        for copy in to_sib(i):
            copy.wait_send()
    for kk in range(2):
        for bb in range(2):
            @pl.when(jnp.logical_not(z_self(kk, bb)))
            def _():
                z_copy(kk, bb).wait_send()

            @pl.when(jnp.logical_not(y2_self(kk, bb)))
            def _():
                y2_copy(kk, bb).wait_send()

        @pl.when(jnp.logical_not(diag_self(kk)))
        def _():
            diag_copy(kk).wait_send()
    for n in range(1, 8):
        y_copy(n).wait_send()

    @pl.when(sums_z)
    def _():
        def z2_left(there, _):
            @pl.when(jnp.logical_not(z2_self(there)))
            def _():
                z2_copy(there).wait_send()
            return 0
        lax.fori_loop(0, 8, z2_left, 0)

    def share_left(i, _):
        share_copy(i).wait_send()
        return 0
    lax.fori_loop(1, 16, share_left, 0)

    def share_on_left(i, _):
        share_on(i).wait_send()
        return 0
    lax.fori_loop(0, 16, share_on_left, 0)

    @pl.when(sums_diag)
    def _():
        def diag_left(k, _):
            diag_back(k).wait_send()
            return 0
        lax.fori_loop(1, 32, diag_left, 0)

    def out_left(n, _):
        @pl.when(jnp.logical_not(out_here(n)))
        def _():
            out_copy(n).wait_send()
        return 0
    lax.fori_loop(0, 8, out_left, 0)

    def out_on_left(n, _):
        out_on(lax.div(n, 4), 2 * lax.rem(n, 4) + c).wait_send()
        return 0
    lax.fori_loop(0, 8, out_on_left, 0)


def on_device(features, gradients, route_ids, gate_share, token_mask, damping):
    route = route_ids.T
    share = gate_share.reshape(1, TOKENS_HERE)
    mask = token_mask.reshape(1, TOKENS_HERE)
    damp = jnp.broadcast_to(damping.reshape(2, 1), (2, 128))
    dma = pltpu.SemaphoreType.DMA
    out = pl.pallas_call(
        refresh,
        out_shape=jax.ShapeDtypeStruct((2, 8, 8, BLOCK), F32),
        in_specs=[pl.BlockSpec(memory_space=pltpu.HBM)] * 6,
        out_specs=pl.BlockSpec(memory_space=pltpu.VMEM),
        scratch_shapes=[
            pltpu.VMEM((2, TOKENS_HERE), jnp.int32),
            pltpu.VMEM((1, TOKENS_HERE), F32),
            pltpu.VMEM((1, TOKENS_HERE), jnp.int32),
            pltpu.VMEM((2, 128), F32),
            pltpu.VMEM((8, TOKENS_HERE, BLOCK), BF16),
            pltpu.VMEM((8, 8, TOKENS_HERE), F32),
            pltpu.VMEM((TOKENS_HERE, BLOCK), BF16),
            pltpu.VMEM((8, TOKENS_HERE), F32),
            pltpu.VMEM((2, 2 * TOKENS_HERE, BLOCK), BF16),
            pltpu.VMEM((2, 3, HALF, HALF), F32),
            pltpu.VMEM((2, 16, 16, HALF), BF16),
            pltpu.VMEM((8, 2, 2, 16, HALF), BF16),
            pltpu.VMEM((2, 8, 128), F32),
            pltpu.VMEM((8, 8, 16, HALF), BF16),
            pltpu.VMEM((8, 2, 2, 16, HALF), BF16),
            pltpu.VMEM((8, 16, HALF), F32),
            pltpu.VMEM((2, 2, 16, HALF), F32),
            pltpu.VMEM((8, 16, HALF), F32),
            pltpu.VMEM((64, 8, 128), F32),
            pltpu.VMEM((2, 16, 16, HALF), F32),
            pltpu.VMEM((8, 128), F32),
            pltpu.VMEM((BLOCK, BLOCK), BF16),
            pltpu.VMEM((BLOCK, BLOCK), BF16),
            pltpu.VMEM((2, 8, BLOCK), F32),
            dma((6,)), dma((3,)), dma((8,)), dma((3,)), dma((8,)), dma((4,)), dma((4,)),
            pltpu.SemaphoreType.REGULAR,
            dma((2, 2)), dma((8,)), dma((8,)), dma((8,)), dma((8,)), dma((2, 2)), dma((8,)),
            dma((2,)), dma, dma((32,)), dma,
            dma((16,)), dma((2, 16)), dma((16,)), dma((8,)), dma((16,)), dma((8,)),
        ],
        compiler_params=pltpu.CompilerParams(
            collective_id=0, has_side_effects=True, vmem_limit_bytes=40 * 1024 * 1024
        ),
    )(features, gradients, route, share, mask, damp)
    return out[0].reshape(8, 1, 8, BLOCK), out[1].reshape(8, 1, 8, BLOCK)


def solution(mesh):
    placed = (
        P(("expert", "dp"), None),
        P(("expert", "dp"), None),
        P(("expert", "dp"), None),
        P(("expert", "dp")),
        P(("expert", "dp")),
        P("expert", None, None),
    )
    return jax.shard_map(
        on_device,
        mesh=mesh,
        in_specs=placed,
        out_specs=(P(None, None, "dp", None), P(None, None, "dp", None)),
        check_vma=False,
    )
```

```python
import jax
import jax.numpy as jnp
from jax import lax
from jax.experimental import pallas as pl
from jax.experimental.pallas import tpu as pltpu
from jax.sharding import PartitionSpec as P

MESH = pl.DeviceIdType.MESH
BLOCK = 512
HALF = 256
TOKENS_HERE = 128
HERE_HALF = 64
LOAD_INVERSE = 1.0 / 16384.0
F32 = jnp.float32
BF16 = jnp.bfloat16


def device_at(x, y, z, c):
    return {"expert": lax.rem(z, 4) * 2 + c, "dp": x * 16 + y * 2 + lax.div(z, 4)}


def split_dot(rows, high, low):
    top = rows.astype(BF16)
    rest = (rows - top.astype(F32)).astype(BF16)
    both = jnp.concatenate([top, rest], axis=0)
    first = jnp.dot(both, high, preferred_element_type=F32)
    second = jnp.dot(top, low, preferred_element_type=F32)
    count = rows.shape[0]
    return first[:count] + (first[count:] + second)


def refresh(
    feat, grad, route_in, share_in, mask_in, damp_in, out,
    route, share, mask, damp,
    tok, wts, other, other_w, spread, gram, corners, folds, diag_out,
    by_z, by_y, z_sums, y_sums, last, diag_y, diag_mid, diag_parts,
    total, diag_total, high, low, rows_out,
    load_sem, tok_send, near_recv, sib_recv, wts_send, wts_recv, both_in,
    z_send, z_recv, y_send, y_recv, z2_send, y2_send, last_recv,
    diag_send, diag_y_recv, diag_mid_send, diag_recv, diag_back_send, diag_back_recv,
    share_send, share_recv, on_send, on_recv, out_send, out_recv, out_on_send, out_on_recv,
):
    expert_at, dp_at = lax.axis_index("expert"), lax.axis_index("dp")
    c, zl = lax.rem(expert_at, 2), lax.div(expert_at, 2)
    zh, y, x = lax.rem(dp_at, 2), lax.rem(lax.div(dp_at, 2), 8), lax.div(dp_at, 16)
    z = zh * 4 + zl
    j, b = lax.div(z, 2), lax.rem(z, 2)
    sib = 1 - c
    parity, half_x = lax.rem(x, 2), lax.div(x, 2)
    mate = x + 1 - 2 * parity
    cross = 3 - x
    row_me = b * 8 + y
    sums_diag = (y == 0) & (b == 0) & (c == 1)
    sums_z = c == lax.rem(j, 2)
    out_self = (half_x == c) & (b == zh)
    sibling = {"expert": expert_at + 1 - 2 * c, "dp": dp_at}

    def remote(src, dst, send, recv, where):
        return pltpu.make_async_remote_copy(
            src_ref=src, dst_ref=dst, send_sem=send, recv_sem=recv,
            device_id=where, device_id_type=MESH,
        )

    leaving = []

    def wait_bytes(like, sem):
        pltpu.make_async_copy(like, like, sem).wait()

    loads = (
        (route_in, route), (share_in, share), (mask_in, mask), (damp_in, damp),
    )
    for n, (src, dst) in enumerate(loads):
        pltpu.make_async_copy(src, dst, load_sem.at[n]).start()

    @pl.when(x < 2)
    def _():
        pltpu.make_async_copy(feat, tok.at[0], load_sem.at[4]).start()
        pltpu.make_async_copy(grad, other, load_sem.at[5]).start()

    @pl.when(x >= 2)
    def _():
        pltpu.make_async_copy(grad, tok.at[0], load_sem.at[4]).start()
        pltpu.make_async_copy(feat, other, load_sem.at[5]).start()

    barrier = pltpu.get_barrier_semaphore()

    def greet(where):
        pl.semaphore_signal(barrier, inc=1, device_id=where, device_id_type=MESH)

    greet(device_at(mate, y, z, c))
    greet(device_at(cross, y, z, c))
    greet(sibling)
    for n in range(1, 8):
        greet({"expert": expert_at, "dp": x * 16 + lax.rem(y + n, 8) * 2 + zh})
        greet(device_at(x, y, lax.rem(z + n, 8), c))

    for n, (src, dst) in enumerate(loads):
        pltpu.make_async_copy(src, dst, load_sem.at[n]).wait()
    lanes = lax.broadcasted_iota(jnp.int32, (8, TOKENS_HERE), 0)
    keep = jnp.broadcast_to(mask[...].astype(F32), (8, TOKENS_HERE))
    is_first = route[0:1, :] == lanes
    is_second = route[1:2, :] == lanes
    share_b = jnp.broadcast_to(share[...], (8, TOKENS_HERE))
    weight_act = jnp.where(is_first | is_second, keep, 0.0)
    weight_grad = jnp.where(is_first, share_b * keep, jnp.where(is_second, (1.0 - share_b) * keep, 0.0))

    @pl.when(x < 2)
    def _():
        wts[0] = weight_act
        other_w[...] = weight_grad

    @pl.when(x >= 2)
    def _():
        wts[0] = weight_grad
        other_w[...] = weight_act

    pltpu.make_async_copy(feat, tok.at[0], load_sem.at[4]).wait()
    pltpu.make_async_copy(grad, other, load_sem.at[5]).wait()
    pl.semaphore_wait(barrier, 17)
    pl.semaphore_signal(both_in, inc=1, device_id=sibling, device_id_type=MESH)

    at_cross, at_mate = device_at(cross, y, z, c), device_at(mate, y, z, c)

    def rows_of(ref, h):
        return ref.at[pl.ds(HERE_HALF * h, HERE_HALF)]

    def to_cross(h):
        return remote(rows_of(other, h), rows_of(tok.at[1], h), tok_send, near_recv.at[0, h], at_cross)

    def to_mate(h):
        return remote(rows_of(tok.at[0], h), rows_of(tok.at[2], h), tok_send, near_recv.at[1, h], at_mate)

    def on_mate(h):
        return remote(rows_of(tok.at[1], h), rows_of(tok.at[3], h), tok_send, near_recv.at[2, h], at_mate)

    def to_sib(i, h):
        return remote(
            rows_of(tok.at[i], h), rows_of(tok.at[4 + i], h), tok_send, sib_recv.at[i], sibling
        )

    to_cross_w = remote(other_w, wts.at[1], wts_send, wts_recv.at[0], at_cross)
    to_mate_w = remote(wts.at[0], wts.at[2], wts_send, wts_recv.at[1], at_mate)
    on_mate_w = remote(wts.at[1], wts.at[3], wts_send, wts_recv.at[2], at_mate)

    def to_sib_w(i):
        return remote(wts.at[i], wts.at[4 + i], wts_send, wts_recv.at[3 + i], sibling)

    def started(copy):
        copy.start()

    def from_sib(i):
        wait_bytes(tok.at[i], sib_recv.at[i])
        to_sib_w(i).wait_recv()

    leaving.append(lambda: wait_bytes(tok.at[pl.ds(0, 7)], tok_send))
    leaving.append(lambda: wait_bytes(wts.at[pl.ds(0, 7)], wts_send))

    def gather_gram(i, begin):
        for kk in range(2):
            e = 4 * parity + 2 * kk + c
            for h, slot in enumerate((i, 4 + i)):
                row = wts[slot, pl.ds(e, 1), :]
                column = jnp.transpose(jnp.broadcast_to(row, (TOKENS_HERE, TOKENS_HERE)))
                for q in range(4):
                    piece = tok[slot, :, 128 * q : 128 * q + 128].astype(F32) * column
                    spread[kk, 128 * h : 128 * h + 128, 128 * q : 128 * q + 128] = piece.astype(BF16)
            left, right = spread[kk, :, :HALF], spread[kk, :, HALF:]
            for n, (one, two) in enumerate(((left, right), (left, left), (right, right))):
                term = lax.dot_general(one, two, (((0,), (0,)), ((), ())), preferred_element_type=F32)
                gram[kk, n] = term if begin else gram[kk, n] + term

    started(to_cross_w)
    started(to_mate_w)
    for h in range(2):
        started(to_cross(h))
        started(to_mate(h))
    for h in range(2):
        started(to_sib(0, h))
    started(to_sib_w(0))
    to_cross_w.wait_recv()
    started(on_mate_w)
    started(to_sib_w(1))
    for h in range(2):
        to_cross(h).wait_recv()
        started(on_mate(h))
        started(to_sib(1, h))
    from_sib(0)
    gather_gram(0, True)
    to_mate_w.wait_recv()
    started(to_sib_w(2))
    for h in range(2):
        to_mate(h).wait_recv()
        started(to_sib(2, h))
    from_sib(1)
    gather_gram(1, False)
    on_mate_w.wait_recv()
    started(to_sib_w(3))
    on_mate(0).wait_recv()
    started(to_sib(3, 0))
    from_sib(2)
    gather_gram(2, False)
    on_mate(1).wait_recv()
    started(to_sib(3, 1))
    from_sib(3)
    gather_gram(3, False)

    pl.semaphore_wait(both_in, 1)

    def z_there(q):
        return 4 * lax.div(q, 2) + 2 * c + lax.rem(q, 2)

    def z_copy(q):
        return remote(
            corners.at[q], by_z.at[z], z_send, z_recv, device_at(x, y, z_there(q), c)
        )

    def y_line(there):
        return {"expert": expert_at, "dp": x * 16 + there * 2 + zh}

    def y_copy(n):
        there = lax.rem(y + n, 8)
        return remote(folds.at[there], by_y.at[y], y_send, y_recv, y_line(there))

    def own_z():
        return pltpu.make_async_copy(corners.at[2 * lax.div(z, 4) + b], by_z.at[z], z_recv)

    def own_y():
        return pltpu.make_async_copy(folds.at[y], by_y.at[y], y_recv)

    r_half = lax.broadcasted_iota(jnp.int32, (HALF, HALF), 0)
    c_half = lax.broadcasted_iota(jnp.int32, (HALF, HALF), 1)
    on_diag = r_half == c_half
    damp_row = jnp.broadcast_to(jnp.where(x < 2, damp[:, 0:1], damp[:, 1:2]), (1, 128))
    for kk in range(2):
        corners[2 * kk : 2 * kk + 2] = gram[kk, 0].astype(BF16).reshape(2, 8, 16, HALF)
        upper, lower = gram[kk, 1], gram[kk, 2]
        folded = jnp.where(r_half <= c_half, upper, lower).astype(BF16)
        folds[:, kk] = folded.reshape(8, 2, 16, HALF)
        d_up = jnp.sum(jnp.where(on_diag, upper, 0.0), axis=0, keepdims=True)
        d_low = jnp.sum(jnp.where(on_diag, lower, 0.0), axis=0, keepdims=True)
        mine = (expert_at == 4 * parity + 2 * kk + c) & (y == 0) & (zh == 0)
        diag_out[kk, 0:1] = d_up[:, :128]
        diag_out[kk, 1:2] = d_up[:, 128:]
        diag_out[kk, 2:3] = d_low[:, :128]
        diag_out[kk, 3:4] = d_low[:, 128:]
        diag_out[kk, 4:8] = jnp.broadcast_to(jnp.where(mine, damp_row, 0.0), (4, 128))

    def diag_copy():
        return remote(diag_out, diag_y.at[y], diag_send, diag_y_recv, y_line(0))

    @pl.when(y != 0)
    def _():
        diag_copy().start()

    def diag_left():
        @pl.when(y != 0)
        def _():
            diag_copy().wait_send()
    leaving.append(diag_left)

    def z_start(n):
        q = lax.rem(j + n, 4)

        @pl.when(z_there(q) != z)
        def _():
            z_copy(q).start()

    def first_left():
        wait_bytes(folds.at[pl.ds(0, 7)], y_send)

        @pl.when(sums_z)
        def _():
            wait_bytes(corners.at[pl.ds(0, 3)], z_send)

        @pl.when(jnp.logical_not(sums_z))
        def _():
            wait_bytes(corners, z_send)
    leaving.append(first_left)

    for n, ahead in enumerate(((4, 1, 7), (3, 5), (2, 6), ())):
        z_start(n)
        for m in ahead:
            started(y_copy(m))
    own_y().start()

    @pl.when(sums_z)
    def _():
        own_z().start()

    wait_bytes(by_y, y_recv)
    sum_y = by_y[0].astype(F32)
    for n in range(1, 8):
        sum_y = sum_y + by_y[n].astype(F32)
    y_sums[...] = sum_y

    def y2_copy(kk, bb):
        return remote(
            y_sums.at[kk, bb], last.at[z], y2_send, last_recv,
            device_at(x, y, 4 * kk + 2 * c + bb, 1),
        )

    def y2_self(kk, bb):
        return (c == 1) & (z == 4 * kk + 2 * c + bb)

    for kk in range(2):
        for bb in range(2):
            @pl.when(jnp.logical_not(y2_self(kk, bb)))
            def _():
                y2_copy(kk, bb).start()

            @pl.when(y2_self(kk, bb))
            def _():
                pltpu.make_async_copy(y_sums.at[kk, bb], last.at[z], last_recv).start()

    def y2_left():
        @pl.when((c == 1) & sums_z)
        def _():
            wait_bytes(last.at[pl.ds(0, 3)], y2_send)

        @pl.when(jnp.logical_not((c == 1) & sums_z))
        def _():
            wait_bytes(last.at[pl.ds(0, 4)], y2_send)
    leaving.append(y2_left)

    def diag_mid_copy(kk):
        return remote(
            diag_mid.at[kk], diag_parts.at[z], diag_mid_send.at[kk], diag_recv,
            device_at(x, 0, 4 * kk + 2 * c, 1),
        )

    def diag_self(kk):
        return (c == 1) & (z == 4 * kk + 2)

    def when_line(step):
        for kk in range(2):
            @pl.when(jnp.logical_not(diag_self(kk)))
            def _():
                step(kk)

    @pl.when(y == 0)
    def _():
        arrived = diag_y.at[pl.ds(1, 7)]
        pltpu.make_async_copy(arrived, arrived, diag_y_recv).wait()
        diag_sum = diag_out[...]
        for n in range(1, 8):
            diag_sum = diag_sum + diag_y[n]
        diag_mid[...] = diag_sum
        when_line(lambda kk: diag_mid_copy(kk).start())
        for kk in range(2):
            @pl.when(diag_self(kk))
            def _():
                pltpu.make_async_copy(diag_mid.at[kk], diag_parts.at[z], diag_recv).start()

    def diag_mid_left():
        @pl.when(y == 0)
        def _():
            when_line(lambda kk: diag_mid_copy(kk).wait_send())
    leaving.append(diag_mid_left)

    def z2_copy(there):
        return remote(
            z_sums.at[there], last.at[y], z2_send, last_recv,
            device_at(x, there, z, 0),
        )

    def z2_self(there):
        return (c == 0) & (there == y)

    @pl.when(sums_z)
    def _():
        wait_bytes(by_z, z_recv)
        sum_z = by_z[0].astype(F32)
        for n in range(1, 8):
            sum_z = sum_z + by_z[n].astype(F32)
        z_sums[...] = sum_z

        def z2_start(n, _):
            there = lax.rem(y + n, 8)

            @pl.when(jnp.logical_not(z2_self(there)))
            def _():
                z2_copy(there).start()

            @pl.when(z2_self(there))
            def _():
                pltpu.make_async_copy(z_sums.at[there], last.at[y], last_recv).start()
            return 0
        lax.fori_loop(0, 8, z2_start, 0)

    def z2_left():
        @pl.when(sums_z & (c == 0))
        def _():
            wait_bytes(z_sums.at[pl.ds(0, 7)], z2_send)

        @pl.when(sums_z & (c == 1))
        def _():
            wait_bytes(z_sums, z2_send)
    leaving.append(z2_left)

    wait_bytes(last, last_recv)
    summed = last[0]
    for n in range(1, 8):
        summed = summed + last[n]
    total[c, row_me] = summed

    def block_line(n, across):
        there = lax.rem(y + n, 8)
        return {"expert": expert_at + across * (2 - 4 * b), "dp": x * 16 + there * 2 + zh}

    def share_copy(n, across):
        own = total.at[c, row_me]
        return remote(own, own, share_send, share_recv.at[b], block_line(n, across))

    def share_on(g):
        group = total.at[c, pl.ds(8 * g, 8)]
        return remote(group, group, on_send.at[g], on_recv.at[g], sibling)

    def diag_to(where):
        return remote(diag_total, diag_total, diag_back_send, diag_back_recv, where)

    block = [(n, across) for n in (4, 3, 5, 2, 6, 1, 7) for across in (1, 0)] + [(0, 1)]
    for n, across in block:
        share_copy(n, across).start()

    @pl.when(sums_diag)
    def _():
        wait_bytes(diag_parts, diag_recv)
        diag_total[...] = jnp.sum(diag_parts[...], axis=0)
        for n, across in block:
            diag_to(block_line(n, across)).start()

    @pl.when(jnp.logical_not(sums_diag))
    def _():
        wait_bytes(diag_total, diag_back_recv)

    @pl.when(c == 1)
    def _():
        diag_to(sibling).start()

    wait_bytes(total.at[c, pl.ds(0, 7)], share_recv.at[b])
    share_on(b).start()
    wait_bytes(total.at[c, pl.ds(0, 8)], share_recv.at[1 - b])
    share_on(1 - b).start()
    for g in range(2):
        group = total.at[sib, pl.ds(8 * g, 8)]
        wait_bytes(group, on_recv.at[g])

    def share_left():
        wait_bytes(total.at[0, pl.ds(0, 15)], share_send)
        for g in range(2):
            share_on(g).wait_send()

        @pl.when(sums_diag)
        def _():
            wait_bytes(diag_y, diag_back_send)

        @pl.when((c == 1) & jnp.logical_not(sums_diag))
        def _():
            wait_bytes(diag_total, diag_back_send)
    leaving.append(share_left)

    corner = total[0].reshape(HALF, HALF) * LOAD_INVERSE
    folded = jnp.concatenate([total[1, 8 * (n % 2) + n // 2] for n in range(16)], axis=0) * LOAD_INVERSE
    turned = jnp.transpose(folded)
    damping = diag_total[4:5, :]
    d_up = jnp.concatenate(
        [diag_total[0:1] * LOAD_INVERSE + damping, diag_total[1:2] * LOAD_INVERSE + damping], axis=1
    )
    d_low = jnp.concatenate(
        [diag_total[2:3] * LOAD_INVERSE + damping, diag_total[3:4] * LOAD_INVERSE + damping], axis=1
    )
    upper = jnp.where(r_half < c_half, folded, jnp.where(r_half > c_half, turned, d_up))
    lower = jnp.where(r_half > c_half, folded, jnp.where(r_half < c_half, turned, d_low))
    corner_turned = jnp.transpose(corner)
    sums_left = jnp.sum(jnp.abs(upper) + jnp.abs(corner_turned), axis=0, keepdims=True)
    sums_right = jnp.sum(jnp.abs(corner) + jnp.abs(lower), axis=0, keepdims=True)
    largest = jnp.max(jnp.maximum(sums_left, sums_right), axis=1, keepdims=True)
    scale = 1.0 / largest
    one = jnp.where(r_half == c_half, 1.0, 0.0)
    for block, at in (
        (one - scale * upper, (slice(0, HALF), slice(0, HALF))),
        (-scale * corner, (slice(0, HALF), slice(HALF, BLOCK))),
        (-scale * corner_turned, (slice(HALF, BLOCK), slice(0, HALF))),
        (one - scale * lower, (slice(HALF, BLOCK), slice(HALF, BLOCK))),
    ):
        top = block.astype(BF16)
        high[at] = top
        low[at] = (block - top.astype(F32)).astype(BF16)

    row_at = lax.broadcasted_iota(jnp.int32, (16, BLOCK), 0)
    col_at = lax.broadcasted_iota(jnp.int32, (16, BLOCK), 1)
    wanted = 8 * (16 * (2 * c + lax.div(row_at, 8)) + 2 * y + b) + lax.rem(row_at, 8)
    unit = jnp.where(col_at == wanted, 1.0, 0.0)
    lead = unit
    for _ in range(7):
        lead = unit + split_dot(lead, high[...], low[...])
    result = lead * scale
    rows_out[0] = result[:8]
    rows_out[1] = result[8:]

    e_me = 4 * parity + j

    def out_copy(n):
        i, zt = n // 4, 4 * b + n % 4
        return remote(
            rows_out.at[i], out.at[half_x, e_me], out_send, out_recv, device_at(2 * c + i, y, zt, half_x)
        )

    def out_here(n):
        return (2 * c + n // 4 == x) & (4 * b + n % 4 == z) & (half_x == c)

    for n in range(8):
        @pl.when(jnp.logical_not(out_here(n)))
        def _():
            out_copy(n).start()

        @pl.when(out_here(n))
        def _():
            pltpu.make_async_copy(rows_out.at[n // 4], out.at[half_x, e_me], out_recv).start()

    wait_bytes(out.at[c], out_recv)
    out_on = remote(out.at[c], out.at[c], out_on_send, out_on_recv, sibling)
    out_on.start()
    wait_bytes(out.at[sib], out_on_recv)

    def out_left():
        @pl.when(out_self)
        def _():
            wait_bytes(out.at[0, pl.ds(0, 7)], out_send)

        @pl.when(jnp.logical_not(out_self))
        def _():
            wait_bytes(out.at[0], out_send)
        out_on.wait_send()
    leaving.append(out_left)

    for left in leaving:
        left()


def on_device(features, gradients, route_ids, gate_share, token_mask, damping):
    route = route_ids.T
    share = gate_share.reshape(1, TOKENS_HERE)
    mask = token_mask.reshape(1, TOKENS_HERE)
    damp = damping.reshape(1, 2)
    dma = pltpu.SemaphoreType.DMA
    out = pl.pallas_call(
        refresh,
        out_shape=jax.ShapeDtypeStruct((2, 8, 8, BLOCK), F32),
        in_specs=[pl.BlockSpec(memory_space=pltpu.HBM)] * 6,
        out_specs=pl.BlockSpec(memory_space=pltpu.VMEM),
        scratch_shapes=[
            pltpu.VMEM((2, TOKENS_HERE), jnp.int32),
            pltpu.VMEM((1, TOKENS_HERE), F32),
            pltpu.VMEM((1, TOKENS_HERE), jnp.int32),
            pltpu.VMEM((1, 2), F32),
            pltpu.VMEM((8, TOKENS_HERE, BLOCK), BF16),
            pltpu.VMEM((8, 8, TOKENS_HERE), F32),
            pltpu.VMEM((TOKENS_HERE, BLOCK), BF16),
            pltpu.VMEM((8, TOKENS_HERE), F32),
            pltpu.VMEM((2, 2 * TOKENS_HERE, BLOCK), BF16),
            pltpu.VMEM((2, 3, HALF, HALF), F32),
            pltpu.VMEM((4, 8, 16, HALF), BF16),
            pltpu.VMEM((8, 2, 2, 16, HALF), BF16),
            pltpu.VMEM((2, 8, 128), F32),
            pltpu.VMEM((8, 8, 16, HALF), BF16),
            pltpu.VMEM((8, 2, 2, 16, HALF), BF16),
            pltpu.VMEM((8, 16, HALF), F32),
            pltpu.VMEM((2, 2, 16, HALF), F32),
            pltpu.VMEM((8, 16, HALF), F32),
            pltpu.VMEM((8, 2, 8, 128), F32),
            pltpu.VMEM((2, 8, 128), F32),
            pltpu.VMEM((8, 8, 128), F32),
            pltpu.VMEM((2, 16, 16, HALF), F32),
            pltpu.VMEM((8, 128), F32),
            pltpu.VMEM((BLOCK, BLOCK), BF16),
            pltpu.VMEM((BLOCK, BLOCK), BF16),
            pltpu.VMEM((2, 8, BLOCK), F32),
            dma((6,)), dma, dma((3, 2)), dma((4,)), dma, dma((7,)), pltpu.SemaphoreType.REGULAR,
            dma, dma, dma, dma, dma, dma, dma,
            dma, dma, dma((2,)), dma, dma, dma,
            dma, dma((2,)), dma((2,)), dma((2,)), dma, dma, dma, dma,
        ],
        compiler_params=pltpu.CompilerParams(
            collective_id=0, has_side_effects=True, vmem_limit_bytes=56 * 1024 * 1024
        ),
    )(features, gradients, route, share, mask, damp)
    return out[0].reshape(8, 1, 8, BLOCK), out[1].reshape(8, 1, 8, BLOCK)


def solution(mesh):
    placed = (
        P(("expert", "dp"), None),
        P(("expert", "dp"), None),
        P(("expert", "dp"), None),
        P(("expert", "dp")),
        P(("expert", "dp")),
        P("expert", None, None),
    )
    return jax.shard_map(
        on_device,
        mesh=mesh,
        in_specs=placed,
        out_specs=(P(None, None, "dp", None), P(None, None, "dp", None)),
        check_vma=False,
    )
```

```python
import jax
import jax.numpy as jnp
from jax import lax
from jax.experimental import pallas as pl
from jax.experimental.pallas import tpu as pltpu
from jax.sharding import PartitionSpec as P

MESH = pl.DeviceIdType.MESH
BLOCK = 512
HALF = 256
TOKENS_HERE = 128
HERE_HALF = 64
LOAD_INVERSE = 1.0 / 16384.0
F32 = jnp.float32
BF16 = jnp.bfloat16


def device_at(x, y, z, c):
    return {"expert": lax.rem(z, 4) * 2 + c, "dp": x * 16 + y * 2 + lax.div(z, 4)}


def split_dot(rows, high, low):
    top = rows.astype(BF16)
    rest = (rows - top.astype(F32)).astype(BF16)
    both = jnp.concatenate([top, rest], axis=0)
    first = jnp.dot(both, high, preferred_element_type=F32)
    second = jnp.dot(top, low, preferred_element_type=F32)
    count = rows.shape[0]
    return first[:count] + (first[count:] + second)


def refresh(
    feat, grad, route_in, share_in, mask_in, damp_in, out,
    route, share, mask, damp,
    tok, wts, other, other_w, spread, gram, corners, folds, diag_out,
    by_z, by_y, z_sums, y_sums, last, diag_y, diag_mid, diag_parts,
    total, diag_total, high, low, rows_out,
    load_sem, tok_send, near_recv, sib_recv, wts_send, wts_recv,
    near_in, lines_in, both_in, cross_in, mate_in,
    z_send, z_recv, y_send, y_recv, z2_send, y2_send, last_recv,
    diag_send, diag_y_recv, diag_mid_send, diag_recv, diag_back_send, diag_back_recv,
    share_send, share_recv, on_send, on_recv, out_send, out_recv, out_on_send, out_on_recv,
):
    expert_at, dp_at = lax.axis_index("expert"), lax.axis_index("dp")
    c, zl = lax.rem(expert_at, 2), lax.div(expert_at, 2)
    zh, y, x = lax.rem(dp_at, 2), lax.rem(lax.div(dp_at, 2), 8), lax.div(dp_at, 16)
    z = zh * 4 + zl
    j, b = lax.div(z, 2), lax.rem(z, 2)
    sib = 1 - c
    parity, half_x = lax.rem(x, 2), lax.div(x, 2)
    mate = x + 1 - 2 * parity
    cross = 3 - x
    row_me = b * 8 + y
    sums_diag = (y == 0) & (b == 0) & (c == 1)
    sums_z = c == lax.rem(j, 2)
    out_self = (half_x == c) & (b == zh)
    sibling = {"expert": expert_at + 1 - 2 * c, "dp": dp_at}

    def remote(src, dst, send, recv, where):
        return pltpu.make_async_remote_copy(
            src_ref=src, dst_ref=dst, send_sem=send, recv_sem=recv,
            device_id=where, device_id_type=MESH,
        )

    leaving = []

    def wait_bytes(like, sem):
        pltpu.make_async_copy(like, like, sem).wait()

    loads = (
        (route_in, route), (share_in, share), (mask_in, mask), (damp_in, damp),
    )
    for n, (src, dst) in enumerate(loads):
        pltpu.make_async_copy(src, dst, load_sem.at[n]).start()

    @pl.when(x < 2)
    def _():
        pltpu.make_async_copy(feat, tok.at[0], load_sem.at[4]).start()
        pltpu.make_async_copy(grad, other, load_sem.at[5]).start()

    @pl.when(x >= 2)
    def _():
        pltpu.make_async_copy(grad, tok.at[0], load_sem.at[4]).start()
        pltpu.make_async_copy(feat, other, load_sem.at[5]).start()

    barrier = pltpu.get_barrier_semaphore()

    def y_line(there):
        return {"expert": expert_at, "dp": x * 16 + there * 2 + zh}

    def near(step):
        return (
            y_line(lax.rem(y + step, 8)), y_line(lax.rem(y + 8 - step, 8)),
            device_at(x, y, lax.rem(z + step, 8), c), device_at(x, y, lax.rem(z + 8 - step, 8), c),
        )

    def tell(sem, where):
        pl.semaphore_signal(sem, inc=1, device_id=where, device_id_type=MESH)

    at_cross, at_mate = device_at(cross, y, z, c), device_at(mate, y, z, c)
    for where in (at_cross, at_mate, *near(1), sibling):
        tell(barrier, where)

    for n, (src, dst) in enumerate(loads):
        pltpu.make_async_copy(src, dst, load_sem.at[n]).wait()
    lanes = lax.broadcasted_iota(jnp.int32, (8, TOKENS_HERE), 0)
    keep = jnp.broadcast_to(mask[...].astype(F32), (8, TOKENS_HERE))
    is_first = route[0:1, :] == lanes
    is_second = route[1:2, :] == lanes
    share_b = jnp.broadcast_to(share[...], (8, TOKENS_HERE))
    weight_act = jnp.where(is_first | is_second, keep, 0.0)
    weight_grad = jnp.where(is_first, share_b * keep, jnp.where(is_second, (1.0 - share_b) * keep, 0.0))

    @pl.when(x < 2)
    def _():
        wts[0] = weight_act
        other_w[...] = weight_grad

    @pl.when(x >= 2)
    def _():
        wts[0] = weight_grad
        other_w[...] = weight_act

    pltpu.make_async_copy(feat, tok.at[0], load_sem.at[4]).wait()
    pltpu.make_async_copy(grad, other, load_sem.at[5]).wait()
    pl.semaphore_wait(barrier, 7)


    def rows_of(ref, h):
        return ref.at[pl.ds(HERE_HALF * h, HERE_HALF)]

    def to_cross(h):
        return remote(rows_of(other, h), rows_of(tok.at[1], h), tok_send, near_recv.at[0, h], at_cross)

    def to_mate(h):
        return remote(rows_of(tok.at[0], h), rows_of(tok.at[2], h), tok_send, near_recv.at[1, h], at_mate)

    def on_mate(h):
        return remote(rows_of(tok.at[1], h), rows_of(tok.at[3], h), tok_send, near_recv.at[2, h], at_mate)

    def to_sib(i, h):
        return remote(
            rows_of(tok.at[i], h), rows_of(tok.at[4 + i], h), tok_send, sib_recv.at[i], sibling
        )

    to_cross_w = remote(other_w, wts.at[1], wts_send, wts_recv.at[0], at_cross)
    to_mate_w = remote(wts.at[0], wts.at[2], wts_send, wts_recv.at[1], at_mate)
    on_mate_w = remote(wts.at[1], wts.at[3], wts_send, wts_recv.at[2], at_mate)

    def to_sib_w(i):
        return remote(wts.at[i], wts.at[4 + i], wts_send, wts_recv.at[3 + i], sibling)

    def started(copy):
        copy.start()

    def from_sib(i):
        wait_bytes(tok.at[i], sib_recv.at[i])
        to_sib_w(i).wait_recv()

    leaving.append(lambda: wait_bytes(tok.at[pl.ds(0, 7)], tok_send))
    leaving.append(lambda: wait_bytes(wts.at[pl.ds(0, 7)], wts_send))

    def gather_gram(i, begin):
        for kk in range(2):
            e = 4 * parity + 2 * kk + c
            for h, slot in enumerate((i, 4 + i)):
                row = wts[slot, pl.ds(e, 1), :]
                column = jnp.transpose(jnp.broadcast_to(row, (TOKENS_HERE, TOKENS_HERE)))
                for q in range(4):
                    piece = tok[slot, :, 128 * q : 128 * q + 128].astype(F32) * column
                    spread[kk, 128 * h : 128 * h + 128, 128 * q : 128 * q + 128] = piece.astype(BF16)
            left, right = spread[kk, :, :HALF], spread[kk, :, HALF:]
            for n, (one, two) in enumerate(((left, right), (left, left), (right, right))):
                term = lax.dot_general(one, two, (((0,), (0,)), ((), ())), preferred_element_type=F32)
                gram[kk, n] = term if begin else gram[kk, n] + term

    started(to_cross_w)
    started(to_mate_w)
    for h in range(2):
        started(to_cross(h))
        started(to_mate(h))
    for h in range(2):
        started(to_sib(0, h))
    started(to_sib_w(0))
    for where in near(1):
        tell(near_in, where)
    to_cross_w.wait_recv()
    started(on_mate_w)
    started(to_sib_w(1))
    for h in range(2):
        to_cross(h).wait_recv()
        started(on_mate(h))
        started(to_sib(1, h))
    from_sib(0)
    gather_gram(0, True)
    to_mate_w.wait_recv()
    started(to_sib_w(2))
    for h in range(2):
        to_mate(h).wait_recv()
        started(to_sib(2, h))
    pl.semaphore_wait(near_in, 4)
    for where in near(2):
        tell(lines_in, where)
    from_sib(1)
    gather_gram(1, False)
    on_mate_w.wait_recv()
    started(to_sib_w(3))
    on_mate(0).wait_recv()
    started(to_sib(3, 0))
    from_sib(2)
    gather_gram(2, False)
    on_mate(1).wait_recv()
    started(to_sib(3, 1))
    from_sib(3)
    gather_gram(3, False)

    pl.semaphore_wait(lines_in, 4)
    tell(both_in, sibling)

    def z_there(q):
        return 4 * lax.div(q, 2) + 2 * c + lax.rem(q, 2)

    def z_copy(q):
        return remote(
            corners.at[q], by_z.at[z], z_send, z_recv, device_at(x, y, z_there(q), c)
        )

    def y_copy(n):
        there = lax.rem(y + n, 8)
        return remote(folds.at[there], by_y.at[y], y_send, y_recv, y_line(there))

    def own_z():
        return pltpu.make_async_copy(corners.at[2 * lax.div(z, 4) + b], by_z.at[z], z_recv)

    def own_y():
        return pltpu.make_async_copy(folds.at[y], by_y.at[y], y_recv)

    r_half = lax.broadcasted_iota(jnp.int32, (HALF, HALF), 0)
    c_half = lax.broadcasted_iota(jnp.int32, (HALF, HALF), 1)
    on_diag = r_half == c_half
    damp_row = jnp.broadcast_to(jnp.where(x < 2, damp[:, 0:1], damp[:, 1:2]), (1, 128))
    for kk in range(2):
        corners[2 * kk : 2 * kk + 2] = gram[kk, 0].astype(BF16).reshape(2, 8, 16, HALF)
        upper, lower = gram[kk, 1], gram[kk, 2]
        folded = jnp.where(r_half <= c_half, upper, lower).astype(BF16)
        folds[:, kk] = folded.reshape(8, 2, 16, HALF)
        d_up = jnp.sum(jnp.where(on_diag, upper, 0.0), axis=0, keepdims=True)
        d_low = jnp.sum(jnp.where(on_diag, lower, 0.0), axis=0, keepdims=True)
        mine = (expert_at == 4 * parity + 2 * kk + c) & (y == 0) & (zh == 0)
        diag_out[kk, 0:1] = d_up[:, :128]
        diag_out[kk, 1:2] = d_up[:, 128:]
        diag_out[kk, 2:3] = d_low[:, :128]
        diag_out[kk, 3:4] = d_low[:, 128:]
        diag_out[kk, 4:8] = jnp.broadcast_to(jnp.where(mine, damp_row, 0.0), (4, 128))

    def diag_copy():
        return remote(diag_out, diag_y.at[y], diag_send, diag_y_recv, y_line(0))

    @pl.when(y != 0)
    def _():
        diag_copy().start()

    def diag_left():
        @pl.when(y != 0)
        def _():
            diag_copy().wait_send()
    leaving.append(diag_left)

    def z_start(n):
        q = lax.rem(j + n, 4)

        @pl.when(z_there(q) != z)
        def _():
            z_copy(q).start()

    def first_left():
        wait_bytes(folds.at[pl.ds(0, 7)], y_send)

        @pl.when(sums_z)
        def _():
            wait_bytes(corners.at[pl.ds(0, 3)], z_send)

        @pl.when(jnp.logical_not(sums_z))
        def _():
            wait_bytes(corners, z_send)
    leaving.append(first_left)

    for n, ahead in enumerate(((4, 1, 7), (3, 5), (2, 6), ())):
        z_start(n)
        for m in ahead:
            started(y_copy(m))
    own_y().start()

    @pl.when(sums_z)
    def _():
        own_z().start()

    pl.semaphore_wait(both_in, 1)
    tell(cross_in, at_cross)
    tell(cross_in, at_mate)
    wait_bytes(by_y, y_recv)
    sum_y = by_y[0].astype(F32)
    for n in range(1, 8):
        sum_y = sum_y + by_y[n].astype(F32)
    y_sums[...] = sum_y

    def y2_copy(kk, bb):
        return remote(
            y_sums.at[kk, bb], last.at[z], y2_send, last_recv,
            device_at(x, y, 4 * kk + 2 * c + bb, 1),
        )

    def y2_self(kk, bb):
        return (c == 1) & (z == 4 * kk + 2 * c + bb)

    for kk in range(2):
        for bb in range(2):
            @pl.when(jnp.logical_not(y2_self(kk, bb)))
            def _():
                y2_copy(kk, bb).start()

            @pl.when(y2_self(kk, bb))
            def _():
                pltpu.make_async_copy(y_sums.at[kk, bb], last.at[z], last_recv).start()

    def y2_left():
        @pl.when((c == 1) & sums_z)
        def _():
            wait_bytes(last.at[pl.ds(0, 3)], y2_send)

        @pl.when(jnp.logical_not((c == 1) & sums_z))
        def _():
            wait_bytes(last.at[pl.ds(0, 4)], y2_send)
    leaving.append(y2_left)

    def diag_mid_copy(kk):
        return remote(
            diag_mid.at[kk], diag_parts.at[z], diag_mid_send.at[kk], diag_recv,
            device_at(x, 0, 4 * kk + 2 * c, 1),
        )

    def diag_self(kk):
        return (c == 1) & (z == 4 * kk + 2)

    def when_line(step):
        for kk in range(2):
            @pl.when(jnp.logical_not(diag_self(kk)))
            def _():
                step(kk)

    @pl.when(y == 0)
    def _():
        arrived = diag_y.at[pl.ds(1, 7)]
        pltpu.make_async_copy(arrived, arrived, diag_y_recv).wait()
        diag_sum = diag_out[...]
        for n in range(1, 8):
            diag_sum = diag_sum + diag_y[n]
        diag_mid[...] = diag_sum
        when_line(lambda kk: diag_mid_copy(kk).start())
        for kk in range(2):
            @pl.when(diag_self(kk))
            def _():
                pltpu.make_async_copy(diag_mid.at[kk], diag_parts.at[z], diag_recv).start()

    def diag_mid_left():
        @pl.when(y == 0)
        def _():
            when_line(lambda kk: diag_mid_copy(kk).wait_send())
    leaving.append(diag_mid_left)

    def z2_copy(there):
        return remote(
            z_sums.at[there], last.at[y], z2_send, last_recv,
            device_at(x, there, z, 0),
        )

    def z2_self(there):
        return (c == 0) & (there == y)

    @pl.when(sums_z)
    def _():
        wait_bytes(by_z, z_recv)
        sum_z = by_z[0].astype(F32)
        for n in range(1, 8):
            sum_z = sum_z + by_z[n].astype(F32)
        z_sums[...] = sum_z

        def z2_start(n, _):
            there = lax.rem(y + n, 8)

            @pl.when(jnp.logical_not(z2_self(there)))
            def _():
                z2_copy(there).start()

            @pl.when(z2_self(there))
            def _():
                pltpu.make_async_copy(z_sums.at[there], last.at[y], last_recv).start()
            return 0
        lax.fori_loop(0, 8, z2_start, 0)

    def z2_left():
        @pl.when(sums_z & (c == 0))
        def _():
            wait_bytes(z_sums.at[pl.ds(0, 7)], z2_send)

        @pl.when(sums_z & (c == 1))
        def _():
            wait_bytes(z_sums, z2_send)
    leaving.append(z2_left)

    wait_bytes(last, last_recv)
    summed = last[0]
    for n in range(1, 8):
        summed = summed + last[n]
    total[c, row_me] = summed

    def block_line(n, across):
        there = lax.rem(y + n, 8)
        return {"expert": expert_at + across * (2 - 4 * b), "dp": x * 16 + there * 2 + zh}

    def share_copy(n, across):
        own = total.at[c, row_me]
        return remote(own, own, share_send, share_recv.at[b], block_line(n, across))

    def share_on(g):
        group = total.at[c, pl.ds(8 * g, 8)]
        return remote(group, group, on_send.at[g], on_recv.at[g], sibling)

    def diag_to(where):
        return remote(diag_total, diag_total, diag_back_send, diag_back_recv, where)

    pl.semaphore_wait(cross_in, 2)
    tell(mate_in, at_mate)
    block = [(n, across) for n in (4, 3, 5, 2, 6, 1, 7) for across in (1, 0)] + [(0, 1)]
    for n, across in block:
        share_copy(n, across).start()

    @pl.when(sums_diag)
    def _():
        wait_bytes(diag_parts, diag_recv)
        diag_total[...] = jnp.sum(diag_parts[...], axis=0)
        for n, across in block:
            diag_to(block_line(n, across)).start()

    @pl.when(jnp.logical_not(sums_diag))
    def _():
        wait_bytes(diag_total, diag_back_recv)

    @pl.when(c == 1)
    def _():
        diag_to(sibling).start()

    wait_bytes(total.at[c, pl.ds(0, 7)], share_recv.at[b])
    share_on(b).start()
    wait_bytes(total.at[c, pl.ds(0, 8)], share_recv.at[1 - b])
    share_on(1 - b).start()
    for g in range(2):
        group = total.at[sib, pl.ds(8 * g, 8)]
        wait_bytes(group, on_recv.at[g])

    def share_left():
        wait_bytes(total.at[0, pl.ds(0, 15)], share_send)
        for g in range(2):
            share_on(g).wait_send()

        @pl.when(sums_diag)
        def _():
            wait_bytes(diag_y, diag_back_send)

        @pl.when((c == 1) & jnp.logical_not(sums_diag))
        def _():
            wait_bytes(diag_total, diag_back_send)
    leaving.append(share_left)

    corner = total[0].reshape(HALF, HALF) * LOAD_INVERSE
    folded = jnp.concatenate([total[1, 8 * (n % 2) + n // 2] for n in range(16)], axis=0) * LOAD_INVERSE
    turned = jnp.transpose(folded)
    damping = diag_total[4:5, :]
    d_up = jnp.concatenate(
        [diag_total[0:1] * LOAD_INVERSE + damping, diag_total[1:2] * LOAD_INVERSE + damping], axis=1
    )
    d_low = jnp.concatenate(
        [diag_total[2:3] * LOAD_INVERSE + damping, diag_total[3:4] * LOAD_INVERSE + damping], axis=1
    )
    upper = jnp.where(r_half < c_half, folded, jnp.where(r_half > c_half, turned, d_up))
    lower = jnp.where(r_half > c_half, folded, jnp.where(r_half < c_half, turned, d_low))
    corner_turned = jnp.transpose(corner)
    sums_left = jnp.sum(jnp.abs(upper) + jnp.abs(corner_turned), axis=0, keepdims=True)
    sums_right = jnp.sum(jnp.abs(corner) + jnp.abs(lower), axis=0, keepdims=True)
    largest = jnp.max(jnp.maximum(sums_left, sums_right), axis=1, keepdims=True)
    scale = 1.0 / largest
    one = jnp.where(r_half == c_half, 1.0, 0.0)
    for block, at in (
        (one - scale * upper, (slice(0, HALF), slice(0, HALF))),
        (-scale * corner, (slice(0, HALF), slice(HALF, BLOCK))),
        (-scale * corner_turned, (slice(HALF, BLOCK), slice(0, HALF))),
        (one - scale * lower, (slice(HALF, BLOCK), slice(HALF, BLOCK))),
    ):
        top = block.astype(BF16)
        high[at] = top
        low[at] = (block - top.astype(F32)).astype(BF16)

    row_at = lax.broadcasted_iota(jnp.int32, (16, BLOCK), 0)
    col_at = lax.broadcasted_iota(jnp.int32, (16, BLOCK), 1)
    wanted = 8 * (16 * (2 * c + lax.div(row_at, 8)) + 2 * y + b) + lax.rem(row_at, 8)
    unit = jnp.where(col_at == wanted, 1.0, 0.0)
    lead = unit
    for _ in range(7):
        lead = unit + split_dot(lead, high[...], low[...])
    result = lead * scale
    rows_out[0] = result[:8]
    rows_out[1] = result[8:]

    pl.semaphore_wait(mate_in, 1)
    e_me = 4 * parity + j

    def out_copy(n):
        i, zt = n // 4, 4 * b + n % 4
        return remote(
            rows_out.at[i], out.at[half_x, e_me], out_send, out_recv, device_at(2 * c + i, y, zt, half_x)
        )

    def out_here(n):
        return (2 * c + n // 4 == x) & (4 * b + n % 4 == z) & (half_x == c)

    for n in range(8):
        @pl.when(jnp.logical_not(out_here(n)))
        def _():
            out_copy(n).start()

        @pl.when(out_here(n))
        def _():
            pltpu.make_async_copy(rows_out.at[n // 4], out.at[half_x, e_me], out_recv).start()

    wait_bytes(out.at[c], out_recv)
    out_on = remote(out.at[c], out.at[c], out_on_send, out_on_recv, sibling)
    out_on.start()
    wait_bytes(out.at[sib], out_on_recv)

    def out_left():
        @pl.when(out_self)
        def _():
            wait_bytes(out.at[0, pl.ds(0, 7)], out_send)

        @pl.when(jnp.logical_not(out_self))
        def _():
            wait_bytes(out.at[0], out_send)
        out_on.wait_send()
    leaving.append(out_left)

    for left in leaving:
        left()


def on_device(features, gradients, route_ids, gate_share, token_mask, damping):
    route = route_ids.T
    share = gate_share.reshape(1, TOKENS_HERE)
    mask = token_mask.reshape(1, TOKENS_HERE)
    damp = damping.reshape(1, 2)
    dma = pltpu.SemaphoreType.DMA
    out = pl.pallas_call(
        refresh,
        out_shape=jax.ShapeDtypeStruct((2, 8, 8, BLOCK), F32),
        in_specs=[pl.BlockSpec(memory_space=pltpu.HBM)] * 6,
        out_specs=pl.BlockSpec(memory_space=pltpu.VMEM),
        scratch_shapes=[
            pltpu.VMEM((2, TOKENS_HERE), jnp.int32),
            pltpu.VMEM((1, TOKENS_HERE), F32),
            pltpu.VMEM((1, TOKENS_HERE), jnp.int32),
            pltpu.VMEM((1, 2), F32),
            pltpu.VMEM((8, TOKENS_HERE, BLOCK), BF16),
            pltpu.VMEM((8, 8, TOKENS_HERE), F32),
            pltpu.VMEM((TOKENS_HERE, BLOCK), BF16),
            pltpu.VMEM((8, TOKENS_HERE), F32),
            pltpu.VMEM((2, 2 * TOKENS_HERE, BLOCK), BF16),
            pltpu.VMEM((2, 3, HALF, HALF), F32),
            pltpu.VMEM((4, 8, 16, HALF), BF16),
            pltpu.VMEM((8, 2, 2, 16, HALF), BF16),
            pltpu.VMEM((2, 8, 128), F32),
            pltpu.VMEM((8, 8, 16, HALF), BF16),
            pltpu.VMEM((8, 2, 2, 16, HALF), BF16),
            pltpu.VMEM((8, 16, HALF), F32),
            pltpu.VMEM((2, 2, 16, HALF), F32),
            pltpu.VMEM((8, 16, HALF), F32),
            pltpu.VMEM((8, 2, 8, 128), F32),
            pltpu.VMEM((2, 8, 128), F32),
            pltpu.VMEM((8, 8, 128), F32),
            pltpu.VMEM((2, 16, 16, HALF), F32),
            pltpu.VMEM((8, 128), F32),
            pltpu.VMEM((BLOCK, BLOCK), BF16),
            pltpu.VMEM((BLOCK, BLOCK), BF16),
            pltpu.VMEM((2, 8, BLOCK), F32),
            dma((6,)), dma, dma((3, 2)), dma((4,)), dma, dma((7,)),
            *[pltpu.SemaphoreType.REGULAR] * 5,
            dma, dma, dma, dma, dma, dma, dma,
            dma, dma, dma((2,)), dma, dma, dma,
            dma, dma((2,)), dma((2,)), dma((2,)), dma, dma, dma, dma,
        ],
        compiler_params=pltpu.CompilerParams(
            collective_id=0, has_side_effects=True, vmem_limit_bytes=40 * 1024 * 1024
        ),
    )(*[pltpu.with_memory_space_constraint(a, pltpu.HBM) for a in (features, gradients, route, share, mask, damp)])
    return out[0].reshape(8, 1, 8, BLOCK), out[1].reshape(8, 1, 8, BLOCK)


def solution(mesh):
    placed = (
        P(("expert", "dp"), None),
        P(("expert", "dp"), None),
        P(("expert", "dp"), None),
        P(("expert", "dp")),
        P(("expert", "dp")),
        P("expert", None, None),
    )
    return jax.shard_map(
        on_device,
        mesh=mesh,
        in_specs=placed,
        out_specs=(P(None, None, "dp", None), P(None, None, "dp", None)),
        check_vma=False,
    )
```

```python
import jax
import jax.numpy as jnp
from jax import lax
from jax.experimental import pallas as pl
from jax.experimental.pallas import tpu as pltpu
from jax.sharding import PartitionSpec as P

MESH = pl.DeviceIdType.MESH
BLOCK = 512
HALF = 256
TOKENS_HERE = 128
HERE_HALF = 64
LOAD_INVERSE = 1.0 / 16384.0
F32 = jnp.float32
BF16 = jnp.bfloat16


def device_at(x, y, z, c):
    return {"expert": lax.rem(z, 4) * 2 + c, "dp": x * 16 + y * 2 + lax.div(z, 4)}


def split_dot(rows, high, low):
    top = rows.astype(BF16)
    rest = (rows - top.astype(F32)).astype(BF16)
    both = jnp.concatenate([top, rest], axis=0)
    first = jnp.dot(both, high, preferred_element_type=F32)
    second = jnp.dot(top, low, preferred_element_type=F32)
    count = rows.shape[0]
    return first[:count] + (first[count:] + second)


def refresh(
    feat, grad, route_in, share_in, mask_in, damp_in, out,
    route, share, mask, damp,
    tok, wts, other, other_w, spread, gram, corners, folds, diag_out,
    by_z, by_y, z_sums, y_sums, last, diag_y, diag_mid, diag_parts,
    total, diag_total, high, low, rows_out,
    load_sem, tok_send, near_recv, sib_recv, wts_send, wts_recv,
    near_in, lines_in, both_in, cross_in, mate_in,
    z_send, z_recv, y_send, y_recv, z2_send, y2_send, last_recv,
    diag_send, diag_y_recv, diag_mid_send, diag_recv, diag_back_send, diag_back_recv,
    share_send, share_recv, on_send, on_recv, out_send, out_recv, out_on_send, out_on_recv,
):
    expert_at, dp_at = lax.axis_index("expert"), lax.axis_index("dp")
    c, zl = lax.rem(expert_at, 2), lax.div(expert_at, 2)
    zh, y, x = lax.rem(dp_at, 2), lax.rem(lax.div(dp_at, 2), 8), lax.div(dp_at, 16)
    z = zh * 4 + zl
    j, b = lax.div(z, 2), lax.rem(z, 2)
    sib = 1 - c
    parity, half_x = lax.rem(x, 2), lax.div(x, 2)
    mate = x + 1 - 2 * parity
    cross = 3 - x
    row_me = b * 8 + y
    sums_diag = (y == 0) & (b == 0) & (c == 1)
    sums_z = c == lax.rem(j, 2)
    out_self = (half_x == c) & (b == zh)
    sibling = {"expert": expert_at + 1 - 2 * c, "dp": dp_at}

    def remote(src, dst, send, recv, where):
        return pltpu.make_async_remote_copy(
            src_ref=src, dst_ref=dst, send_sem=send, recv_sem=recv,
            device_id=where, device_id_type=MESH,
        )

    leaving = []

    def wait_bytes(like, sem):
        pltpu.make_async_copy(like, like, sem).wait()

    loads = (
        (route_in, route), (share_in, share), (mask_in, mask), (damp_in, damp),
    )
    for n, (src, dst) in enumerate(loads):
        pltpu.make_async_copy(src, dst, load_sem.at[n]).start()

    @pl.when(x < 2)
    def _():
        pltpu.make_async_copy(feat, tok.at[0], load_sem.at[4]).start()
        pltpu.make_async_copy(grad, other, load_sem.at[5]).start()

    @pl.when(x >= 2)
    def _():
        pltpu.make_async_copy(grad, tok.at[0], load_sem.at[4]).start()
        pltpu.make_async_copy(feat, other, load_sem.at[5]).start()

    barrier = pltpu.get_barrier_semaphore()
    z_end, y_end = (z == 3) | (z == 4), (y == 3) | (y == 4)
    ends = z_end.astype(jnp.int32) + y_end.astype(jnp.int32)

    def y_line(there):
        return {"expert": expert_at, "dp": x * 16 + there * 2 + zh}

    def tell(sem, where):
        pl.semaphore_signal(sem, inc=1, device_id=where, device_id_type=MESH)

    z_four = [{"expert": lax.rem(zl + n, 4) * 2 + c, "dp": dp_at} for n in range(1, 4)]
    y_four = [y_line(4 * lax.div(y, 4) + lax.rem(y + n, 4)) for n in range(1, 4)]
    at_cross, at_mate = device_at(cross, y, z, c), device_at(mate, y, z, c)

    def tell_over(sem):
        @pl.when(z_end)
        def _():
            tell(sem, device_at(x, y, 7 - z, c))

        @pl.when(y_end)
        def _():
            tell(sem, y_line(7 - y))

    tell_over(barrier)
    for where in (*z_four, *y_four, at_cross, at_mate, sibling):
        tell(barrier, where)

    for n, (src, dst) in enumerate(loads):
        pltpu.make_async_copy(src, dst, load_sem.at[n]).wait()
    lanes = lax.broadcasted_iota(jnp.int32, (8, TOKENS_HERE), 0)
    keep = jnp.broadcast_to(mask[...].astype(F32), (8, TOKENS_HERE))
    is_first = route[0:1, :] == lanes
    is_second = route[1:2, :] == lanes
    share_b = jnp.broadcast_to(share[...], (8, TOKENS_HERE))
    weight_act = jnp.where(is_first | is_second, keep, 0.0)
    weight_grad = jnp.where(is_first, share_b * keep, jnp.where(is_second, (1.0 - share_b) * keep, 0.0))

    @pl.when(x < 2)
    def _():
        wts[0] = weight_act
        other_w[...] = weight_grad

    @pl.when(x >= 2)
    def _():
        wts[0] = weight_grad
        other_w[...] = weight_act

    pltpu.make_async_copy(feat, tok.at[0], load_sem.at[4]).wait()
    pltpu.make_async_copy(grad, other, load_sem.at[5]).wait()
    pl.semaphore_wait(barrier, 9 + ends)
    tell_over(near_in)


    def rows_of(ref, h):
        return ref.at[pl.ds(HERE_HALF * h, HERE_HALF)]

    def to_cross(h):
        return remote(rows_of(other, h), rows_of(tok.at[1], h), tok_send, near_recv.at[0, h], at_cross)

    def to_mate(h):
        return remote(rows_of(tok.at[0], h), rows_of(tok.at[2], h), tok_send, near_recv.at[1, h], at_mate)

    def on_mate(h):
        return remote(rows_of(tok.at[1], h), rows_of(tok.at[3], h), tok_send, near_recv.at[2, h], at_mate)

    def to_sib(i, h):
        return remote(
            rows_of(tok.at[i], h), rows_of(tok.at[4 + i], h), tok_send, sib_recv.at[i], sibling
        )

    to_cross_w = remote(other_w, wts.at[1], wts_send, wts_recv.at[0], at_cross)
    to_mate_w = remote(wts.at[0], wts.at[2], wts_send, wts_recv.at[1], at_mate)
    on_mate_w = remote(wts.at[1], wts.at[3], wts_send, wts_recv.at[2], at_mate)

    def to_sib_w(i):
        return remote(wts.at[i], wts.at[4 + i], wts_send, wts_recv.at[3 + i], sibling)

    def started(copy):
        copy.start()

    def from_sib(i):
        wait_bytes(tok.at[i], sib_recv.at[i])
        to_sib_w(i).wait_recv()

    leaving.append(lambda: wait_bytes(tok.at[pl.ds(0, 7)], tok_send))
    leaving.append(lambda: wait_bytes(wts.at[pl.ds(0, 7)], wts_send))

    def gather_gram(i, begin):
        for kk in range(2):
            e = 4 * parity + 2 * kk + c
            for h, slot in enumerate((i, 4 + i)):
                row = wts[slot, pl.ds(e, 1), :]
                column = jnp.transpose(jnp.broadcast_to(row, (TOKENS_HERE, TOKENS_HERE)))
                for q in range(4):
                    piece = tok[slot, :, 128 * q : 128 * q + 128].astype(F32) * column
                    spread[kk, 128 * h : 128 * h + 128, 128 * q : 128 * q + 128] = piece.astype(BF16)
            left, right = spread[kk, :, :HALF], spread[kk, :, HALF:]
            for n, (one, two) in enumerate(((left, right), (left, left), (right, right))):
                term = lax.dot_general(one, two, (((0,), (0,)), ((), ())), preferred_element_type=F32)
                gram[kk, n] = term if begin else gram[kk, n] + term

    started(to_cross_w)
    started(to_mate_w)
    for h in range(2):
        started(to_cross(h))
        started(to_mate(h))
    for h in range(2):
        started(to_sib(0, h))
    started(to_sib_w(0))
    to_cross_w.wait_recv()
    started(on_mate_w)
    started(to_sib_w(1))
    for h in range(2):
        to_cross(h).wait_recv()
        started(on_mate(h))
        started(to_sib(1, h))

    @pl.when(ends > 0)
    def _():
        pl.semaphore_wait(near_in, ends)

    @pl.when(z_end)
    def _():
        for where in z_four:
            tell(lines_in, where)

    @pl.when(y_end)
    def _():
        for where in y_four:
            tell(lines_in, where)
    from_sib(0)
    gather_gram(0, True)
    to_mate_w.wait_recv()
    started(to_sib_w(2))
    for h in range(2):
        to_mate(h).wait_recv()
        started(to_sib(2, h))
    from_sib(1)
    gather_gram(1, False)
    on_mate_w.wait_recv()
    started(to_sib_w(3))
    on_mate(0).wait_recv()
    started(to_sib(3, 0))
    from_sib(2)
    gather_gram(2, False)
    on_mate(1).wait_recv()
    started(to_sib(3, 1))
    from_sib(3)
    gather_gram(3, False)

    @pl.when(ends < 2)
    def _():
        pl.semaphore_wait(lines_in, 2 - ends)
    tell(both_in, sibling)

    def z_there(q):
        return 4 * lax.div(q, 2) + 2 * c + lax.rem(q, 2)

    def z_copy(q):
        return remote(
            corners.at[q], by_z.at[z], z_send, z_recv, device_at(x, y, z_there(q), c)
        )

    def y_copy(n):
        there = lax.rem(y + n, 8)
        return remote(folds.at[there], by_y.at[y], y_send, y_recv, y_line(there))

    def own_z():
        return pltpu.make_async_copy(corners.at[2 * lax.div(z, 4) + b], by_z.at[z], z_recv)

    def own_y():
        return pltpu.make_async_copy(folds.at[y], by_y.at[y], y_recv)

    r_half = lax.broadcasted_iota(jnp.int32, (HALF, HALF), 0)
    c_half = lax.broadcasted_iota(jnp.int32, (HALF, HALF), 1)
    on_diag = r_half == c_half
    damp_row = jnp.broadcast_to(jnp.where(x < 2, damp[:, 0:1], damp[:, 1:2]), (1, 128))
    for kk in range(2):
        corners[2 * kk : 2 * kk + 2] = gram[kk, 0].astype(BF16).reshape(2, 8, 16, HALF)
        upper, lower = gram[kk, 1], gram[kk, 2]
        folded = jnp.where(r_half <= c_half, upper, lower).astype(BF16)
        folds[:, kk] = folded.reshape(8, 2, 16, HALF)
        d_up = jnp.sum(jnp.where(on_diag, upper, 0.0), axis=0, keepdims=True)
        d_low = jnp.sum(jnp.where(on_diag, lower, 0.0), axis=0, keepdims=True)
        mine = (expert_at == 4 * parity + 2 * kk + c) & (y == 0) & (zh == 0)
        diag_out[kk, 0:1] = d_up[:, :128]
        diag_out[kk, 1:2] = d_up[:, 128:]
        diag_out[kk, 2:3] = d_low[:, :128]
        diag_out[kk, 3:4] = d_low[:, 128:]
        diag_out[kk, 4:8] = jnp.broadcast_to(jnp.where(mine, damp_row, 0.0), (4, 128))

    def diag_copy():
        return remote(diag_out, diag_y.at[y], diag_send, diag_y_recv, y_line(0))

    @pl.when(y != 0)
    def _():
        diag_copy().start()

    def diag_left():
        @pl.when(y != 0)
        def _():
            diag_copy().wait_send()
    leaving.append(diag_left)

    def z_start(n):
        q = lax.rem(j + n, 4)

        @pl.when(z_there(q) != z)
        def _():
            z_copy(q).start()

    def first_left():
        wait_bytes(folds.at[pl.ds(0, 7)], y_send)

        @pl.when(sums_z)
        def _():
            wait_bytes(corners.at[pl.ds(0, 3)], z_send)

        @pl.when(jnp.logical_not(sums_z))
        def _():
            wait_bytes(corners, z_send)
    leaving.append(first_left)

    for n, ahead in enumerate(((4, 1, 7), (3, 5), (2, 6), ())):
        z_start(n)
        for m in ahead:
            started(y_copy(m))
    own_y().start()

    @pl.when(sums_z)
    def _():
        own_z().start()

    pl.semaphore_wait(both_in, 1)
    tell(cross_in, at_cross)
    tell(cross_in, at_mate)
    wait_bytes(by_y, y_recv)
    sum_y = by_y[0].astype(F32)
    for n in range(1, 8):
        sum_y = sum_y + by_y[n].astype(F32)
    y_sums[...] = sum_y

    def y2_copy(kk, bb):
        return remote(
            y_sums.at[kk, bb], last.at[z], y2_send, last_recv,
            device_at(x, y, 4 * kk + 2 * c + bb, 1),
        )

    def y2_self(kk, bb):
        return (c == 1) & (z == 4 * kk + 2 * c + bb)

    for kk in range(2):
        for bb in range(2):
            @pl.when(jnp.logical_not(y2_self(kk, bb)))
            def _():
                y2_copy(kk, bb).start()

            @pl.when(y2_self(kk, bb))
            def _():
                pltpu.make_async_copy(y_sums.at[kk, bb], last.at[z], last_recv).start()

    def y2_left():
        @pl.when((c == 1) & sums_z)
        def _():
            wait_bytes(last.at[pl.ds(0, 3)], y2_send)

        @pl.when(jnp.logical_not((c == 1) & sums_z))
        def _():
            wait_bytes(last.at[pl.ds(0, 4)], y2_send)
    leaving.append(y2_left)

    def diag_mid_copy(kk):
        return remote(
            diag_mid.at[kk], diag_parts.at[z], diag_mid_send.at[kk], diag_recv,
            device_at(x, 0, 4 * kk + 2 * c, 1),
        )

    def diag_self(kk):
        return (c == 1) & (z == 4 * kk + 2)

    def when_line(step):
        for kk in range(2):
            @pl.when(jnp.logical_not(diag_self(kk)))
            def _():
                step(kk)

    @pl.when(y == 0)
    def _():
        arrived = diag_y.at[pl.ds(1, 7)]
        pltpu.make_async_copy(arrived, arrived, diag_y_recv).wait()
        diag_sum = diag_out[...]
        for n in range(1, 8):
            diag_sum = diag_sum + diag_y[n]
        diag_mid[...] = diag_sum
        when_line(lambda kk: diag_mid_copy(kk).start())
        for kk in range(2):
            @pl.when(diag_self(kk))
            def _():
                pltpu.make_async_copy(diag_mid.at[kk], diag_parts.at[z], diag_recv).start()

    def diag_mid_left():
        @pl.when(y == 0)
        def _():
            when_line(lambda kk: diag_mid_copy(kk).wait_send())
    leaving.append(diag_mid_left)

    def z2_copy(there):
        return remote(
            z_sums.at[there], last.at[y], z2_send, last_recv,
            device_at(x, there, z, 0),
        )

    def z2_self(there):
        return (c == 0) & (there == y)

    @pl.when(sums_z)
    def _():
        wait_bytes(by_z, z_recv)
        sum_z = by_z[0].astype(F32)
        for n in range(1, 8):
            sum_z = sum_z + by_z[n].astype(F32)
        z_sums[...] = sum_z

        def z2_start(n, _):
            there = lax.rem(y + n, 8)

            @pl.when(jnp.logical_not(z2_self(there)))
            def _():
                z2_copy(there).start()

            @pl.when(z2_self(there))
            def _():
                pltpu.make_async_copy(z_sums.at[there], last.at[y], last_recv).start()
            return 0
        lax.fori_loop(0, 8, z2_start, 0)

    def z2_left():
        @pl.when(sums_z & (c == 0))
        def _():
            wait_bytes(z_sums.at[pl.ds(0, 7)], z2_send)

        @pl.when(sums_z & (c == 1))
        def _():
            wait_bytes(z_sums, z2_send)
    leaving.append(z2_left)

    wait_bytes(last, last_recv)
    summed = last[0]
    for n in range(1, 8):
        summed = summed + last[n]
    total[c, row_me] = summed

    def block_line(n, across):
        there = lax.rem(y + n, 8)
        return {"expert": expert_at + across * (2 - 4 * b), "dp": x * 16 + there * 2 + zh}

    def share_copy(n, across):
        own = total.at[c, row_me]
        return remote(own, own, share_send, share_recv.at[b], block_line(n, across))

    def share_on(g):
        group = total.at[c, pl.ds(8 * g, 8)]
        return remote(group, group, on_send.at[g], on_recv.at[g], sibling)

    def diag_to(where):
        return remote(diag_total, diag_total, diag_back_send, diag_back_recv, where)

    pl.semaphore_wait(cross_in, 2)
    tell(mate_in, at_mate)
    block = [(n, across) for n in (4, 3, 5, 2, 6, 1, 7) for across in (1, 0)] + [(0, 1)]
    for n, across in block:
        share_copy(n, across).start()

    @pl.when(sums_diag)
    def _():
        wait_bytes(diag_parts, diag_recv)
        diag_total[...] = jnp.sum(diag_parts[...], axis=0)
        for n, across in block:
            diag_to(block_line(n, across)).start()

    @pl.when(jnp.logical_not(sums_diag))
    def _():
        wait_bytes(diag_total, diag_back_recv)

    @pl.when(c == 1)
    def _():
        diag_to(sibling).start()

    wait_bytes(total.at[c, pl.ds(0, 7)], share_recv.at[b])
    share_on(b).start()
    wait_bytes(total.at[c, pl.ds(0, 8)], share_recv.at[1 - b])
    share_on(1 - b).start()
    for g in range(2):
        group = total.at[sib, pl.ds(8 * g, 8)]
        wait_bytes(group, on_recv.at[g])

    def share_left():
        wait_bytes(total.at[0, pl.ds(0, 15)], share_send)
        for g in range(2):
            share_on(g).wait_send()

        @pl.when(sums_diag)
        def _():
            wait_bytes(diag_y, diag_back_send)

        @pl.when((c == 1) & jnp.logical_not(sums_diag))
        def _():
            wait_bytes(diag_total, diag_back_send)
    leaving.append(share_left)

    corner = total[0].reshape(HALF, HALF) * LOAD_INVERSE
    folded = jnp.concatenate([total[1, 8 * (n % 2) + n // 2] for n in range(16)], axis=0) * LOAD_INVERSE
    turned = jnp.transpose(folded)
    damping = diag_total[4:5, :]
    d_up = jnp.concatenate(
        [diag_total[0:1] * LOAD_INVERSE + damping, diag_total[1:2] * LOAD_INVERSE + damping], axis=1
    )
    d_low = jnp.concatenate(
        [diag_total[2:3] * LOAD_INVERSE + damping, diag_total[3:4] * LOAD_INVERSE + damping], axis=1
    )
    upper = jnp.where(r_half < c_half, folded, jnp.where(r_half > c_half, turned, d_up))
    lower = jnp.where(r_half > c_half, folded, jnp.where(r_half < c_half, turned, d_low))
    corner_turned = jnp.transpose(corner)
    sums_left = jnp.sum(jnp.abs(upper) + jnp.abs(corner_turned), axis=0, keepdims=True)
    sums_right = jnp.sum(jnp.abs(corner) + jnp.abs(lower), axis=0, keepdims=True)
    largest = jnp.max(jnp.maximum(sums_left, sums_right), axis=1, keepdims=True)
    scale = 1.0 / largest
    one = jnp.where(r_half == c_half, 1.0, 0.0)
    for block, at in (
        (one - scale * upper, (slice(0, HALF), slice(0, HALF))),
        (-scale * corner, (slice(0, HALF), slice(HALF, BLOCK))),
        (-scale * corner_turned, (slice(HALF, BLOCK), slice(0, HALF))),
        (one - scale * lower, (slice(HALF, BLOCK), slice(HALF, BLOCK))),
    ):
        top = block.astype(BF16)
        high[at] = top
        low[at] = (block - top.astype(F32)).astype(BF16)

    row_at = lax.broadcasted_iota(jnp.int32, (16, BLOCK), 0)
    col_at = lax.broadcasted_iota(jnp.int32, (16, BLOCK), 1)
    wanted = 8 * (16 * (2 * c + lax.div(row_at, 8)) + 2 * y + b) + lax.rem(row_at, 8)
    unit = jnp.where(col_at == wanted, 1.0, 0.0)
    here = []
    for i in range(2):
        rows = pl.ds(pl.multiple_of(16 * (8 * (2 * c + i) + y), 16), 16)
        both = high[rows, :].astype(F32) + low[rows, :].astype(F32)
        here.append(jnp.where(b == 0, both[:8], both[8:]))
    lead = unit + jnp.concatenate(here, axis=0)
    for _ in range(6):
        lead = unit + split_dot(lead, high[...], low[...])
    result = lead * scale
    rows_out[0] = result[:8]
    rows_out[1] = result[8:]

    pl.semaphore_wait(mate_in, 1)
    e_me = 4 * parity + j

    def out_copy(n):
        i, zt = n // 4, 4 * b + n % 4
        return remote(
            rows_out.at[i], out.at[half_x, e_me], out_send, out_recv, device_at(2 * c + i, y, zt, half_x)
        )

    def out_here(n):
        return (2 * c + n // 4 == x) & (4 * b + n % 4 == z) & (half_x == c)

    for n in range(8):
        @pl.when(jnp.logical_not(out_here(n)))
        def _():
            out_copy(n).start()

        @pl.when(out_here(n))
        def _():
            pltpu.make_async_copy(rows_out.at[n // 4], out.at[half_x, e_me], out_recv).start()

    wait_bytes(out.at[c], out_recv)
    out_on = remote(out.at[c], out.at[c], out_on_send, out_on_recv, sibling)
    out_on.start()
    wait_bytes(out.at[sib], out_on_recv)

    def out_left():
        @pl.when(out_self)
        def _():
            wait_bytes(out.at[0, pl.ds(0, 7)], out_send)

        @pl.when(jnp.logical_not(out_self))
        def _():
            wait_bytes(out.at[0], out_send)
        out_on.wait_send()
    leaving.append(out_left)

    for left in leaving:
        left()


def on_device(features, gradients, route_ids, gate_share, token_mask, damping):
    route = route_ids.T
    share = gate_share.reshape(1, TOKENS_HERE)
    mask = token_mask.reshape(1, TOKENS_HERE)
    damp = damping.reshape(1, 2)
    dma = pltpu.SemaphoreType.DMA
    out = pl.pallas_call(
        refresh,
        out_shape=jax.ShapeDtypeStruct((2, 8, 8, BLOCK), F32),
        in_specs=[pl.BlockSpec(memory_space=pltpu.HBM)] * 6,
        out_specs=pl.BlockSpec(memory_space=pltpu.VMEM),
        scratch_shapes=[
            pltpu.VMEM((2, TOKENS_HERE), jnp.int32),
            pltpu.VMEM((1, TOKENS_HERE), F32),
            pltpu.VMEM((1, TOKENS_HERE), jnp.int32),
            pltpu.VMEM((1, 2), F32),
            pltpu.VMEM((8, TOKENS_HERE, BLOCK), BF16),
            pltpu.VMEM((8, 8, TOKENS_HERE), F32),
            pltpu.VMEM((TOKENS_HERE, BLOCK), BF16),
            pltpu.VMEM((8, TOKENS_HERE), F32),
            pltpu.VMEM((2, 2 * TOKENS_HERE, BLOCK), BF16),
            pltpu.VMEM((2, 3, HALF, HALF), F32),
            pltpu.VMEM((4, 8, 16, HALF), BF16),
            pltpu.VMEM((8, 2, 2, 16, HALF), BF16),
            pltpu.VMEM((2, 8, 128), F32),
            pltpu.VMEM((8, 8, 16, HALF), BF16),
            pltpu.VMEM((8, 2, 2, 16, HALF), BF16),
            pltpu.VMEM((8, 16, HALF), F32),
            pltpu.VMEM((2, 2, 16, HALF), F32),
            pltpu.VMEM((8, 16, HALF), F32),
            pltpu.VMEM((8, 2, 8, 128), F32),
            pltpu.VMEM((2, 8, 128), F32),
            pltpu.VMEM((8, 8, 128), F32),
            pltpu.VMEM((2, 16, 16, HALF), F32),
            pltpu.VMEM((8, 128), F32),
            pltpu.VMEM((BLOCK, BLOCK), BF16),
            pltpu.VMEM((BLOCK, BLOCK), BF16),
            pltpu.VMEM((2, 8, BLOCK), F32),
            dma((6,)), dma, dma((3, 2)), dma((4,)), dma, dma((7,)),
            *[pltpu.SemaphoreType.REGULAR] * 5,
            dma, dma, dma, dma, dma, dma, dma,
            dma, dma, dma((2,)), dma, dma, dma,
            dma, dma((2,)), dma((2,)), dma((2,)), dma, dma, dma, dma,
        ],
        compiler_params=pltpu.CompilerParams(
            collective_id=0, has_side_effects=True, vmem_limit_bytes=40 * 1024 * 1024
        ),
    )(*[pltpu.with_memory_space_constraint(a, pltpu.HBM) for a in (features, gradients, route, share, mask, damp)])
    return out[0].reshape(8, 1, 8, BLOCK), out[1].reshape(8, 1, 8, BLOCK)


def solution(mesh):
    placed = (
        P(("expert", "dp"), None),
        P(("expert", "dp"), None),
        P(("expert", "dp"), None),
        P(("expert", "dp")),
        P(("expert", "dp")),
        P("expert", None, None),
    )
    return jax.shard_map(
        on_device,
        mesh=mesh,
        in_specs=placed,
        out_specs=(P(None, None, "dp", None), P(None, None, "dp", None)),
        check_vma=False,
    )
```

```python
import jax
import jax.numpy as jnp
from jax import lax
from jax.experimental import pallas as pl
from jax.experimental.pallas import tpu as pltpu
from jax.sharding import PartitionSpec as P

MESH = pl.DeviceIdType.MESH
BLOCK = 512
HALF = 256
TOKENS_HERE = 128
HERE_PART = 32
PARTS = 4
LOAD_INVERSE = 1.0 / 16384.0
F32 = jnp.float32
BF16 = jnp.bfloat16


def device_at(x, y, z, c):
    return {"expert": lax.rem(z, 4) * 2 + c, "dp": x * 16 + y * 2 + lax.div(z, 4)}


def split_dot(rows, high, low):
    top = rows.astype(BF16)
    rest = (rows - top.astype(F32)).astype(BF16)
    both = jnp.concatenate([top, rest], axis=0)
    first = jnp.dot(both, high, preferred_element_type=F32)
    second = jnp.dot(top, low, preferred_element_type=F32)
    count = rows.shape[0]
    return first[:count] + (first[count:] + second)


def refresh(
    feat, grad, route_in, share_in, mask_in, damp_in, out,
    route, share, mask, damp,
    tok, wts, other, other_w, spread, gram, corners, folds, diag_out,
    by_z, by_y, z_sums, y_sums, last, diag_y, diag_mid, diag_parts,
    total, diag_total, high, low, rows_out,
    load_sem, tok_send, near_recv, sib_recv, wts_send, wts_recv,
    near_in, lines_in, both_in, cross_in, mate_in,
    z_send, z_recv, y_send, y_recv, z2_send, y2_send, last_recv,
    diag_send, diag_y_recv, diag_mid_send, diag_recv, diag_back_send, diag_back_recv,
    share_send, share_recv, on_send, on_recv, out_send, out_recv, out_on_send, out_on_recv,
):
    expert_at, dp_at = lax.axis_index("expert"), lax.axis_index("dp")
    c, zl = lax.rem(expert_at, 2), lax.div(expert_at, 2)
    zh, y, x = lax.rem(dp_at, 2), lax.rem(lax.div(dp_at, 2), 8), lax.div(dp_at, 16)
    z = zh * 4 + zl
    j, b = lax.div(z, 2), lax.rem(z, 2)
    sib = 1 - c
    parity, half_x = lax.rem(x, 2), lax.div(x, 2)
    mate = x + 1 - 2 * parity
    cross = 3 - x
    row_me = b * 8 + y
    sums_diag = (y == 0) & (b == 0) & (c == 1)
    sums_z = c == lax.rem(j, 2)
    out_self = (half_x == c) & (b == zh)
    sibling = {"expert": expert_at + 1 - 2 * c, "dp": dp_at}

    def remote(src, dst, send, recv, where):
        return pltpu.make_async_remote_copy(
            src_ref=src, dst_ref=dst, send_sem=send, recv_sem=recv,
            device_id=where, device_id_type=MESH,
        )

    leaving = []

    def wait_bytes(like, sem):
        pltpu.make_async_copy(like, like, sem).wait()

    loads = (
        (route_in, route), (share_in, share), (mask_in, mask), (damp_in, damp),
    )
    for n, (src, dst) in enumerate(loads):
        pltpu.make_async_copy(src, dst, load_sem.at[n]).start()

    @pl.when(x < 2)
    def _():
        pltpu.make_async_copy(feat, tok.at[0], load_sem.at[4]).start()
        pltpu.make_async_copy(grad, other, load_sem.at[5]).start()

    @pl.when(x >= 2)
    def _():
        pltpu.make_async_copy(grad, tok.at[0], load_sem.at[4]).start()
        pltpu.make_async_copy(feat, other, load_sem.at[5]).start()

    barrier = pltpu.get_barrier_semaphore()
    z_end, y_end = (z == 3) | (z == 4), (y == 3) | (y == 4)
    ends = z_end.astype(jnp.int32) + y_end.astype(jnp.int32)

    def y_line(there):
        return {"expert": expert_at, "dp": x * 16 + there * 2 + zh}

    def tell(sem, where):
        pl.semaphore_signal(sem, inc=1, device_id=where, device_id_type=MESH)

    z_four = [{"expert": lax.rem(zl + n, 4) * 2 + c, "dp": dp_at} for n in range(1, 4)]
    y_four = [y_line(4 * lax.div(y, 4) + lax.rem(y + n, 4)) for n in range(1, 4)]
    at_cross, at_mate = device_at(cross, y, z, c), device_at(mate, y, z, c)

    def tell_over(sem):
        @pl.when(z_end)
        def _():
            tell(sem, device_at(x, y, 7 - z, c))

        @pl.when(y_end)
        def _():
            tell(sem, y_line(7 - y))

    tell_over(barrier)
    for where in (*z_four, *y_four, at_cross, at_mate, sibling):
        tell(barrier, where)

    for n, (src, dst) in enumerate(loads):
        pltpu.make_async_copy(src, dst, load_sem.at[n]).wait()
    lanes = lax.broadcasted_iota(jnp.int32, (8, TOKENS_HERE), 0)
    keep = jnp.broadcast_to(mask[...].astype(F32), (8, TOKENS_HERE))
    is_first = route[0:1, :] == lanes
    is_second = route[1:2, :] == lanes
    share_b = jnp.broadcast_to(share[...], (8, TOKENS_HERE))
    weight_act = jnp.where(is_first | is_second, keep, 0.0)
    weight_grad = jnp.where(is_first, share_b * keep, jnp.where(is_second, (1.0 - share_b) * keep, 0.0))

    @pl.when(x < 2)
    def _():
        wts[0] = weight_act
        other_w[...] = weight_grad

    @pl.when(x >= 2)
    def _():
        wts[0] = weight_grad
        other_w[...] = weight_act

    pltpu.make_async_copy(feat, tok.at[0], load_sem.at[4]).wait()
    pltpu.make_async_copy(grad, other, load_sem.at[5]).wait()
    pl.semaphore_wait(barrier, 9 + ends)
    tell_over(near_in)


    def rows_of(ref, h):
        return ref.at[pl.ds(HERE_PART * h, HERE_PART)]

    def to_cross(h):
        return remote(rows_of(other, h), rows_of(tok.at[1], h), tok_send, near_recv.at[0, h], at_cross)

    def to_mate(h):
        return remote(rows_of(tok.at[0], h), rows_of(tok.at[2], h), tok_send, near_recv.at[1, h], at_mate)

    def on_mate(h):
        return remote(rows_of(tok.at[1], h), rows_of(tok.at[3], h), tok_send, near_recv.at[2, h], at_mate)

    def to_sib(i, h):
        return remote(
            rows_of(tok.at[i], h), rows_of(tok.at[4 + i], h), tok_send, sib_recv.at[i], sibling
        )

    to_cross_w = remote(other_w, wts.at[1], wts_send, wts_recv.at[0], at_cross)
    to_mate_w = remote(wts.at[0], wts.at[2], wts_send, wts_recv.at[1], at_mate)
    on_mate_w = remote(wts.at[1], wts.at[3], wts_send, wts_recv.at[2], at_mate)

    def to_sib_w(i):
        return remote(wts.at[i], wts.at[4 + i], wts_send, wts_recv.at[3 + i], sibling)

    def started(copy):
        copy.start()

    def from_sib(i):
        wait_bytes(tok.at[i], sib_recv.at[i])
        to_sib_w(i).wait_recv()

    leaving.append(lambda: wait_bytes(tok.at[pl.ds(0, 7)], tok_send))
    leaving.append(lambda: wait_bytes(wts.at[pl.ds(0, 7)], wts_send))

    def gather_gram(i, begin):
        for kk in range(2):
            e = 4 * parity + 2 * kk + c
            for h, slot in enumerate((i, 4 + i)):
                row = wts[slot, pl.ds(e, 1), :]
                column = jnp.transpose(jnp.broadcast_to(row, (TOKENS_HERE, TOKENS_HERE)))
                for q in range(4):
                    piece = tok[slot, :, 128 * q : 128 * q + 128].astype(F32) * column
                    spread[kk, 128 * h : 128 * h + 128, 128 * q : 128 * q + 128] = piece.astype(BF16)
            left, right = spread[kk, :, :HALF], spread[kk, :, HALF:]
            for n, (one, two) in enumerate(((left, right), (left, left), (right, right))):
                term = lax.dot_general(one, two, (((0,), (0,)), ((), ())), preferred_element_type=F32)
                gram[kk, n] = term if begin else gram[kk, n] + term

    started(to_cross_w)
    started(to_mate_w)
    for h in range(PARTS):
        started(to_cross(h))
        started(to_mate(h))
    for h in range(PARTS):
        started(to_sib(0, h))
    started(to_sib_w(0))
    to_cross_w.wait_recv()
    started(on_mate_w)
    started(to_sib_w(1))
    for h in range(PARTS):
        to_cross(h).wait_recv()
        started(on_mate(h))
        started(to_sib(1, h))

    @pl.when(ends > 0)
    def _():
        pl.semaphore_wait(near_in, ends)

    @pl.when(z_end)
    def _():
        for where in z_four:
            tell(lines_in, where)

    @pl.when(y_end)
    def _():
        for where in y_four:
            tell(lines_in, where)
    from_sib(0)
    gather_gram(0, True)
    to_mate_w.wait_recv()
    started(to_sib_w(2))
    for h in range(PARTS):
        to_mate(h).wait_recv()
        started(to_sib(2, h))
    from_sib(1)
    gather_gram(1, False)
    on_mate_w.wait_recv()
    started(to_sib_w(3))
    for h in range(PARTS - 1):
        on_mate(h).wait_recv()
        started(to_sib(3, h))
    from_sib(2)
    gather_gram(2, False)
    on_mate(PARTS - 1).wait_recv()
    started(to_sib(3, PARTS - 1))
    from_sib(3)
    gather_gram(3, False)

    @pl.when(ends < 2)
    def _():
        pl.semaphore_wait(lines_in, 2 - ends)
    tell(both_in, sibling)

    def z_there(q):
        return 4 * lax.div(q, 2) + 2 * c + lax.rem(q, 2)

    def z_copy(q):
        return remote(
            corners.at[q], by_z.at[z], z_send, z_recv, device_at(x, y, z_there(q), c)
        )

    def y_copy(n):
        there = lax.rem(y + n, 8)
        return remote(folds.at[there], by_y.at[y], y_send, y_recv, y_line(there))

    def own_z():
        return pltpu.make_async_copy(corners.at[2 * lax.div(z, 4) + b], by_z.at[z], z_recv)

    def own_y():
        return pltpu.make_async_copy(folds.at[y], by_y.at[y], y_recv)

    r_half = lax.broadcasted_iota(jnp.int32, (HALF, HALF), 0)
    c_half = lax.broadcasted_iota(jnp.int32, (HALF, HALF), 1)
    on_diag = r_half == c_half
    damp_row = jnp.broadcast_to(jnp.where(x < 2, damp[:, 0:1], damp[:, 1:2]), (1, 128))
    for kk in range(2):
        corners[2 * kk : 2 * kk + 2] = gram[kk, 0].astype(BF16).reshape(2, 8, 16, HALF)
        upper, lower = gram[kk, 1], gram[kk, 2]
        folded = jnp.where(r_half <= c_half, upper, lower).astype(BF16)
        folds[:, kk] = folded.reshape(8, 2, 16, HALF)
        d_up = jnp.sum(jnp.where(on_diag, upper, 0.0), axis=0, keepdims=True)
        d_low = jnp.sum(jnp.where(on_diag, lower, 0.0), axis=0, keepdims=True)
        mine = (expert_at == 4 * parity + 2 * kk + c) & (y == 0) & (zh == 0)
        diag_out[kk, 0:1] = d_up[:, :128]
        diag_out[kk, 1:2] = d_up[:, 128:]
        diag_out[kk, 2:3] = d_low[:, :128]
        diag_out[kk, 3:4] = d_low[:, 128:]
        diag_out[kk, 4:8] = jnp.broadcast_to(jnp.where(mine, damp_row, 0.0), (4, 128))

    def diag_copy():
        return remote(diag_out, diag_y.at[y], diag_send, diag_y_recv, y_line(0))

    @pl.when(y != 0)
    def _():
        diag_copy().start()

    def diag_left():
        @pl.when(y != 0)
        def _():
            diag_copy().wait_send()
    leaving.append(diag_left)

    def z_start(n):
        q = lax.rem(j + n, 4)

        @pl.when(z_there(q) != z)
        def _():
            z_copy(q).start()

    def first_left():
        wait_bytes(folds.at[pl.ds(0, 7)], y_send)

        @pl.when(sums_z)
        def _():
            wait_bytes(corners.at[pl.ds(0, 3)], z_send)

        @pl.when(jnp.logical_not(sums_z))
        def _():
            wait_bytes(corners, z_send)
    leaving.append(first_left)

    for n, ahead in enumerate(((4, 1, 7), (3, 5), (2, 6), ())):
        z_start(n)
        for m in ahead:
            started(y_copy(m))
    own_y().start()

    @pl.when(sums_z)
    def _():
        own_z().start()

    pl.semaphore_wait(both_in, 1)
    tell(cross_in, at_cross)
    tell(cross_in, at_mate)
    wait_bytes(by_y, y_recv)
    sum_y = by_y[0].astype(F32)
    for n in range(1, 8):
        sum_y = sum_y + by_y[n].astype(F32)
    y_sums[...] = sum_y

    def y2_copy(kk, bb):
        return remote(
            y_sums.at[kk, bb], last.at[z], y2_send, last_recv,
            device_at(x, y, 4 * kk + 2 * c + bb, 1),
        )

    def y2_self(kk, bb):
        return (c == 1) & (z == 4 * kk + 2 * c + bb)

    for far in range(2):
        kk = (1 - lax.div(z, 4)) if far == 0 else lax.div(z, 4)
        for bb in range(2):
            @pl.when(jnp.logical_not(y2_self(kk, bb)))
            def _():
                y2_copy(kk, bb).start()

            @pl.when(y2_self(kk, bb))
            def _():
                pltpu.make_async_copy(y_sums.at[kk, bb], last.at[z], last_recv).start()

    def y2_left():
        @pl.when((c == 1) & sums_z)
        def _():
            wait_bytes(last.at[pl.ds(0, 3)], y2_send)

        @pl.when(jnp.logical_not((c == 1) & sums_z))
        def _():
            wait_bytes(last.at[pl.ds(0, 4)], y2_send)
    leaving.append(y2_left)

    def z2_copy(there):
        return remote(
            z_sums.at[there], last.at[y], z2_send, last_recv,
            device_at(x, there, z, 0),
        )

    def z2_self(there):
        return (c == 0) & (there == y)

    @pl.when(sums_z)
    def _():
        wait_bytes(by_z, z_recv)
        sum_z = by_z[0].astype(F32)
        for n in range(1, 8):
            sum_z = sum_z + by_z[n].astype(F32)
        z_sums[...] = sum_z

        for n in (4, 3, 5, 2, 6, 1, 7, 0):
            there = lax.rem(y + n, 8)

            @pl.when(jnp.logical_not(z2_self(there)))
            def _():
                z2_copy(there).start()

            @pl.when(z2_self(there))
            def _():
                pltpu.make_async_copy(z_sums.at[there], last.at[y], last_recv).start()

    def diag_mid_copy(kk):
        return remote(
            diag_mid.at[kk], diag_parts.at[z], diag_mid_send.at[kk], diag_recv,
            device_at(x, 0, 4 * kk + 2 * c, 1),
        )

    def diag_self(kk):
        return (c == 1) & (z == 4 * kk + 2)

    def when_line(step):
        for kk in range(2):
            @pl.when(jnp.logical_not(diag_self(kk)))
            def _():
                step(kk)

    @pl.when(y == 0)
    def _():
        arrived = diag_y.at[pl.ds(1, 7)]
        pltpu.make_async_copy(arrived, arrived, diag_y_recv).wait()
        diag_sum = diag_out[...]
        for n in range(1, 8):
            diag_sum = diag_sum + diag_y[n]
        diag_mid[...] = diag_sum
        when_line(lambda kk: diag_mid_copy(kk).start())
        for kk in range(2):
            @pl.when(diag_self(kk))
            def _():
                pltpu.make_async_copy(diag_mid.at[kk], diag_parts.at[z], diag_recv).start()

    def diag_mid_left():
        @pl.when(y == 0)
        def _():
            when_line(lambda kk: diag_mid_copy(kk).wait_send())
    leaving.append(diag_mid_left)

    def z2_left():
        @pl.when(sums_z & (c == 0))
        def _():
            wait_bytes(z_sums.at[pl.ds(0, 7)], z2_send)

        @pl.when(sums_z & (c == 1))
        def _():
            wait_bytes(z_sums, z2_send)
    leaving.append(z2_left)

    wait_bytes(last, last_recv)
    summed = last[0]
    for n in range(1, 8):
        summed = summed + last[n]
    total[c, row_me] = summed

    def block_line(n, across):
        there = lax.rem(y + n, 8)
        return {"expert": expert_at + across * (2 - 4 * b), "dp": x * 16 + there * 2 + zh}

    def share_copy(n, across):
        own = total.at[c, row_me]
        return remote(own, own, share_send, share_recv.at[b], block_line(n, across))

    def share_on(g):
        group = total.at[c, pl.ds(8 * g, 8)]
        return remote(group, group, on_send.at[g], on_recv.at[g], sibling)

    def diag_to(where):
        return remote(diag_total, diag_total, diag_back_send, diag_back_recv, where)

    pl.semaphore_wait(cross_in, 2)
    tell(mate_in, at_mate)
    block = [(n, across) for n in (4, 3, 5, 2, 6, 1, 7) for across in (1, 0)] + [(0, 1)]
    for n, across in block:
        share_copy(n, across).start()

    @pl.when(sums_diag)
    def _():
        wait_bytes(diag_parts, diag_recv)
        diag_total[...] = jnp.sum(diag_parts[...], axis=0)
        for n, across in block:
            diag_to(block_line(n, across)).start()

    @pl.when(jnp.logical_not(sums_diag))
    def _():
        wait_bytes(diag_total, diag_back_recv)

    @pl.when(c == 1)
    def _():
        diag_to(sibling).start()

    wait_bytes(total.at[c, pl.ds(0, 7)], share_recv.at[b])
    share_on(b).start()
    wait_bytes(total.at[c, pl.ds(0, 8)], share_recv.at[1 - b])
    share_on(1 - b).start()
    for g in range(2):
        group = total.at[sib, pl.ds(8 * g, 8)]
        wait_bytes(group, on_recv.at[g])

    def share_left():
        wait_bytes(total.at[0, pl.ds(0, 15)], share_send)
        for g in range(2):
            share_on(g).wait_send()

        @pl.when(sums_diag)
        def _():
            wait_bytes(diag_y, diag_back_send)

        @pl.when((c == 1) & jnp.logical_not(sums_diag))
        def _():
            wait_bytes(diag_total, diag_back_send)
    leaving.append(share_left)

    corner = total[0].reshape(HALF, HALF) * LOAD_INVERSE
    folded = jnp.concatenate([total[1, 8 * (n % 2) + n // 2] for n in range(16)], axis=0) * LOAD_INVERSE
    turned = jnp.transpose(folded)
    damping = diag_total[4:5, :]
    d_up = jnp.concatenate(
        [diag_total[0:1] * LOAD_INVERSE + damping, diag_total[1:2] * LOAD_INVERSE + damping], axis=1
    )
    d_low = jnp.concatenate(
        [diag_total[2:3] * LOAD_INVERSE + damping, diag_total[3:4] * LOAD_INVERSE + damping], axis=1
    )
    upper = jnp.where(r_half < c_half, folded, jnp.where(r_half > c_half, turned, d_up))
    lower = jnp.where(r_half > c_half, folded, jnp.where(r_half < c_half, turned, d_low))
    corner_turned = jnp.transpose(corner)
    sums_left = jnp.sum(jnp.abs(upper) + jnp.abs(corner_turned), axis=0, keepdims=True)
    sums_right = jnp.sum(jnp.abs(corner) + jnp.abs(lower), axis=0, keepdims=True)
    largest = jnp.max(jnp.maximum(sums_left, sums_right), axis=1, keepdims=True)
    scale = 1.0 / largest
    one = jnp.where(r_half == c_half, 1.0, 0.0)
    for block, at in (
        (one - scale * upper, (slice(0, HALF), slice(0, HALF))),
        (-scale * corner, (slice(0, HALF), slice(HALF, BLOCK))),
        (-scale * corner_turned, (slice(HALF, BLOCK), slice(0, HALF))),
        (one - scale * lower, (slice(HALF, BLOCK), slice(HALF, BLOCK))),
    ):
        top = block.astype(BF16)
        high[at] = top
        low[at] = (block - top.astype(F32)).astype(BF16)

    row_at = lax.broadcasted_iota(jnp.int32, (16, BLOCK), 0)
    col_at = lax.broadcasted_iota(jnp.int32, (16, BLOCK), 1)
    wanted = 8 * (16 * (2 * c + lax.div(row_at, 8)) + 2 * y + b) + lax.rem(row_at, 8)
    unit = jnp.where(col_at == wanted, 1.0, 0.0)
    here = []
    for i in range(2):
        rows = pl.ds(pl.multiple_of(16 * (8 * (2 * c + i) + y), 16), 16)
        both = high[rows, :].astype(F32) + low[rows, :].astype(F32)
        here.append(jnp.where(b == 0, both[:8], both[8:]))
    lead = unit + jnp.concatenate(here, axis=0)
    for _ in range(6):
        lead = unit + split_dot(lead, high[...], low[...])
    result = lead * scale
    rows_out[0] = result[:8]
    rows_out[1] = result[8:]

    pl.semaphore_wait(mate_in, 1)
    e_me = 4 * parity + j

    def out_copy(n):
        i, zt = n // 4, 4 * b + n % 4
        return remote(
            rows_out.at[i], out.at[half_x, e_me], out_send, out_recv, device_at(2 * c + i, y, zt, half_x)
        )

    def out_here(n):
        return (2 * c + n // 4 == x) & (4 * b + n % 4 == z) & (half_x == c)

    for n in range(8):
        @pl.when(jnp.logical_not(out_here(n)))
        def _():
            out_copy(n).start()

        @pl.when(out_here(n))
        def _():
            pltpu.make_async_copy(rows_out.at[n // 4], out.at[half_x, e_me], out_recv).start()

    wait_bytes(out.at[c], out_recv)
    out_on = remote(out.at[c], out.at[c], out_on_send, out_on_recv, sibling)
    out_on.start()
    wait_bytes(out.at[sib], out_on_recv)

    def out_left():
        @pl.when(out_self)
        def _():
            wait_bytes(out.at[0, pl.ds(0, 7)], out_send)

        @pl.when(jnp.logical_not(out_self))
        def _():
            wait_bytes(out.at[0], out_send)
        out_on.wait_send()
    leaving.append(out_left)

    for left in leaving:
        left()


def on_device(features, gradients, route_ids, gate_share, token_mask, damping):
    route = route_ids.T
    share = gate_share.reshape(1, TOKENS_HERE)
    mask = token_mask.reshape(1, TOKENS_HERE)
    damp = damping.reshape(1, 2)
    dma = pltpu.SemaphoreType.DMA
    out = pl.pallas_call(
        refresh,
        out_shape=jax.ShapeDtypeStruct((2, 8, 8, BLOCK), F32),
        in_specs=[pl.BlockSpec(memory_space=pltpu.HBM)] * 6,
        out_specs=pl.BlockSpec(memory_space=pltpu.VMEM),
        scratch_shapes=[
            pltpu.VMEM((2, TOKENS_HERE), jnp.int32),
            pltpu.VMEM((1, TOKENS_HERE), F32),
            pltpu.VMEM((1, TOKENS_HERE), jnp.int32),
            pltpu.VMEM((1, 2), F32),
            pltpu.VMEM((8, TOKENS_HERE, BLOCK), BF16),
            pltpu.VMEM((8, 8, TOKENS_HERE), F32),
            pltpu.VMEM((TOKENS_HERE, BLOCK), BF16),
            pltpu.VMEM((8, TOKENS_HERE), F32),
            pltpu.VMEM((2, 2 * TOKENS_HERE, BLOCK), BF16),
            pltpu.VMEM((2, 3, HALF, HALF), F32),
            pltpu.VMEM((4, 8, 16, HALF), BF16),
            pltpu.VMEM((8, 2, 2, 16, HALF), BF16),
            pltpu.VMEM((2, 8, 128), F32),
            pltpu.VMEM((8, 8, 16, HALF), BF16),
            pltpu.VMEM((8, 2, 2, 16, HALF), BF16),
            pltpu.VMEM((8, 16, HALF), F32),
            pltpu.VMEM((2, 2, 16, HALF), F32),
            pltpu.VMEM((8, 16, HALF), F32),
            pltpu.VMEM((8, 2, 8, 128), F32),
            pltpu.VMEM((2, 8, 128), F32),
            pltpu.VMEM((8, 8, 128), F32),
            pltpu.VMEM((2, 16, 16, HALF), F32),
            pltpu.VMEM((8, 128), F32),
            pltpu.VMEM((BLOCK, BLOCK), BF16),
            pltpu.VMEM((BLOCK, BLOCK), BF16),
            pltpu.VMEM((2, 8, BLOCK), F32),
            dma((6,)), dma, dma((3, PARTS)), dma((4,)), dma, dma((7,)),
            *[pltpu.SemaphoreType.REGULAR] * 5,
            dma, dma, dma, dma, dma, dma, dma,
            dma, dma, dma((2,)), dma, dma, dma,
            dma, dma((2,)), dma((2,)), dma((2,)), dma, dma, dma, dma,
        ],
        compiler_params=pltpu.CompilerParams(
            collective_id=0, has_side_effects=True, vmem_limit_bytes=40 * 1024 * 1024
        ),
    )(*[pltpu.with_memory_space_constraint(a, pltpu.HBM) for a in (features, gradients, route, share, mask, damp)])
    return out[0].reshape(8, 1, 8, BLOCK), out[1].reshape(8, 1, 8, BLOCK)


def solution(mesh):
    placed = (
        P(("expert", "dp"), None),
        P(("expert", "dp"), None),
        P(("expert", "dp"), None),
        P(("expert", "dp")),
        P(("expert", "dp")),
        P("expert", None, None),
    )
    return jax.shard_map(
        on_device,
        mesh=mesh,
        in_specs=placed,
        out_specs=(P(None, None, "dp", None), P(None, None, "dp", None)),
        check_vma=False,
    )
```

```python
import jax
import jax.numpy as jnp
from jax import lax
from jax.experimental import pallas as pl
from jax.experimental.pallas import tpu as pltpu
from jax.sharding import PartitionSpec as P

MESH = pl.DeviceIdType.MESH
BLOCK = 512
HALF = 256
TOKENS_HERE = 128
HERE_PART = 32
PARTS = 4
LOAD_INVERSE = 1.0 / 16384.0
F32 = jnp.float32
BF16 = jnp.bfloat16


def device_at(x, y, z, c):
    return {"expert": lax.rem(z, 4) * 2 + c, "dp": x * 16 + y * 2 + lax.div(z, 4)}


def split_dot(rows, high, low):
    top = rows.astype(BF16)
    rest = (rows - top.astype(F32)).astype(BF16)
    both = jnp.concatenate([top, rest], axis=0)
    first = jnp.dot(both, high, preferred_element_type=F32)
    second = jnp.dot(top, low, preferred_element_type=F32)
    count = rows.shape[0]
    return first[:count] + (first[count:] + second)


def refresh(
    feat, grad, route_in, share_in, mask_in, damp_in, out,
    route, share, mask, damp,
    tok, wts, other, other_w, spread, gram, corners, folds, diag_out,
    by_z, by_y, z_sums, y_sums, last, diag_y, diag_mid, diag_parts,
    total, diag_total, high, low, rows_out,
    load_sem, tok_send, near_recv, sib_recv, wts_send, wts_recv,
    near_in, lines_in, both_in, cross_in, mate_in,
    z_send, z_recv, y_send, y_recv, z2_send, y2_send, last_recv,
    diag_send, diag_y_recv, diag_mid_send, diag_recv, diag_back_send, diag_back_recv,
    share_send, share_recv, on_send, on_recv, out_send, out_recv, out_on_send, out_on_recv,
):
    expert_at, dp_at = lax.axis_index("expert"), lax.axis_index("dp")
    c, zl = lax.rem(expert_at, 2), lax.div(expert_at, 2)
    zh, y, x = lax.rem(dp_at, 2), lax.rem(lax.div(dp_at, 2), 8), lax.div(dp_at, 16)
    z = zh * 4 + zl
    j, b = lax.div(z, 2), lax.rem(z, 2)
    sib = 1 - c
    parity, half_x = lax.rem(x, 2), lax.div(x, 2)
    mate = x + 1 - 2 * parity
    cross = 3 - x
    row_me = b * 8 + y
    sums_diag = (y == 0) & (b == 0) & (c == 1)
    sums_z = c == lax.rem(j, 2)
    out_self = (half_x == c) & (b == zh)
    sibling = {"expert": expert_at + 1 - 2 * c, "dp": dp_at}

    def remote(src, dst, send, recv, where):
        return pltpu.make_async_remote_copy(
            src_ref=src, dst_ref=dst, send_sem=send, recv_sem=recv,
            device_id=where, device_id_type=MESH,
        )

    leaving = []

    def wait_bytes(like, sem):
        pltpu.make_async_copy(like, like, sem).wait()

    loads = (
        (route_in, route), (share_in, share), (mask_in, mask), (damp_in, damp),
    )
    for n, (src, dst) in enumerate(loads):
        pltpu.make_async_copy(src, dst, load_sem.at[n]).start()

    @pl.when(x < 2)
    def _():
        pltpu.make_async_copy(feat, tok.at[0], load_sem.at[4]).start()
        pltpu.make_async_copy(grad, other, load_sem.at[5]).start()

    @pl.when(x >= 2)
    def _():
        pltpu.make_async_copy(grad, tok.at[0], load_sem.at[4]).start()
        pltpu.make_async_copy(feat, other, load_sem.at[5]).start()

    barrier = pltpu.get_barrier_semaphore()
    z_end, y_end = (z == 3) | (z == 4), (y == 3) | (y == 4)
    ends = z_end.astype(jnp.int32) + y_end.astype(jnp.int32)

    def y_line(there):
        return {"expert": expert_at, "dp": x * 16 + there * 2 + zh}

    def tell(sem, where):
        pl.semaphore_signal(sem, inc=1, device_id=where, device_id_type=MESH)

    z_four = [{"expert": lax.rem(zl + n, 4) * 2 + c, "dp": dp_at} for n in range(1, 4)]
    y_four = [y_line(4 * lax.div(y, 4) + lax.rem(y + n, 4)) for n in range(1, 4)]
    at_cross, at_mate = device_at(cross, y, z, c), device_at(mate, y, z, c)

    def tell_over(sem):
        @pl.when(z_end)
        def _():
            tell(sem, device_at(x, y, 7 - z, c))

        @pl.when(y_end)
        def _():
            tell(sem, y_line(7 - y))

    tell_over(barrier)
    for where in (*z_four, *y_four, at_cross, at_mate, sibling):
        tell(barrier, where)

    for n, (src, dst) in enumerate(loads):
        pltpu.make_async_copy(src, dst, load_sem.at[n]).wait()
    lanes = lax.broadcasted_iota(jnp.int32, (8, TOKENS_HERE), 0)
    keep = jnp.broadcast_to(mask[...].astype(F32), (8, TOKENS_HERE))
    is_first = route[0:1, :] == lanes
    is_second = route[1:2, :] == lanes
    share_b = jnp.broadcast_to(share[...], (8, TOKENS_HERE))
    weight_act = jnp.where(is_first | is_second, keep, 0.0)
    weight_grad = jnp.where(is_first, share_b * keep, jnp.where(is_second, (1.0 - share_b) * keep, 0.0))

    @pl.when(x < 2)
    def _():
        wts[0] = weight_act
        other_w[...] = weight_grad

    @pl.when(x >= 2)
    def _():
        wts[0] = weight_grad
        other_w[...] = weight_act

    pltpu.make_async_copy(feat, tok.at[0], load_sem.at[4]).wait()
    pltpu.make_async_copy(grad, other, load_sem.at[5]).wait()
    pl.semaphore_wait(barrier, 9 + ends)
    tell_over(near_in)


    def rows_of(ref, h):
        return ref.at[pl.ds(HERE_PART * h, HERE_PART)]

    def to_cross(h):
        return remote(rows_of(other, h), rows_of(tok.at[1], h), tok_send, near_recv.at[0, h], at_cross)

    def to_mate(h):
        return remote(rows_of(tok.at[0], h), rows_of(tok.at[2], h), tok_send, near_recv.at[1, h], at_mate)

    def on_mate(h):
        return remote(rows_of(tok.at[1], h), rows_of(tok.at[3], h), tok_send, near_recv.at[2, h], at_mate)

    def to_sib(i, h):
        return remote(
            rows_of(tok.at[i], h), rows_of(tok.at[4 + i], h), tok_send, sib_recv.at[i], sibling
        )

    to_cross_w = remote(other_w, wts.at[1], wts_send, wts_recv.at[0], at_cross)
    to_mate_w = remote(wts.at[0], wts.at[2], wts_send, wts_recv.at[1], at_mate)
    on_mate_w = remote(wts.at[1], wts.at[3], wts_send, wts_recv.at[2], at_mate)

    def to_sib_w(i):
        return remote(wts.at[i], wts.at[4 + i], wts_send, wts_recv.at[3 + i], sibling)

    def started(copy):
        copy.start()

    def from_sib(i):
        wait_bytes(tok.at[i], sib_recv.at[i])
        to_sib_w(i).wait_recv()

    leaving.append(lambda: wait_bytes(tok.at[pl.ds(0, 7)], tok_send))
    leaving.append(lambda: wait_bytes(wts.at[pl.ds(0, 7)], wts_send))

    def gather_gram(i, begin):
        for kk in range(2):
            e = 4 * parity + 2 * kk + c
            for h, slot in enumerate((i, 4 + i)):
                row = wts[slot, pl.ds(e, 1), :]
                column = jnp.transpose(jnp.broadcast_to(row, (TOKENS_HERE, TOKENS_HERE)))
                for q in range(4):
                    piece = tok[slot, :, 128 * q : 128 * q + 128].astype(F32) * column
                    spread[kk, 128 * h : 128 * h + 128, 128 * q : 128 * q + 128] = piece.astype(BF16)
            left, right = spread[kk, :, :HALF], spread[kk, :, HALF:]
            for n, (one, two) in enumerate(((left, right), (left, left), (right, right))):
                term = lax.dot_general(one, two, (((0,), (0,)), ((), ())), preferred_element_type=F32)
                gram[kk, n] = term if begin else gram[kk, n] + term

    started(to_cross_w)
    started(to_mate_w)
    for h in range(PARTS):
        started(to_cross(h))
    for h in range(PARTS):
        started(to_mate(h))
    for h in range(PARTS):
        started(to_sib(0, h))
    started(to_sib_w(0))
    to_cross_w.wait_recv()
    started(on_mate_w)
    started(to_sib_w(1))
    for h in range(PARTS):
        to_cross(h).wait_recv()
        started(on_mate(h))
        started(to_sib(1, h))

    @pl.when(ends > 0)
    def _():
        pl.semaphore_wait(near_in, ends)

    @pl.when(z_end)
    def _():
        for where in z_four:
            tell(lines_in, where)

    @pl.when(y_end)
    def _():
        for where in y_four:
            tell(lines_in, where)
    from_sib(0)
    gather_gram(0, True)
    to_mate_w.wait_recv()
    started(to_sib_w(2))
    for h in range(PARTS):
        to_mate(h).wait_recv()
        started(to_sib(2, h))
    from_sib(1)
    gather_gram(1, False)
    on_mate_w.wait_recv()
    started(to_sib_w(3))
    for h in range(PARTS - 1):
        on_mate(h).wait_recv()
        started(to_sib(3, h))
    from_sib(2)
    gather_gram(2, False)
    on_mate(PARTS - 1).wait_recv()
    started(to_sib(3, PARTS - 1))
    from_sib(3)
    gather_gram(3, False)

    @pl.when(ends < 2)
    def _():
        pl.semaphore_wait(lines_in, 2 - ends)
    tell(both_in, sibling)

    def z_there(q):
        return 4 * lax.div(q, 2) + 2 * c + lax.rem(q, 2)

    def z_copy(q):
        return remote(
            corners.at[q], by_z.at[z], z_send, z_recv, device_at(x, y, z_there(q), c)
        )

    def y_copy(n):
        there = lax.rem(y + n, 8)
        return remote(folds.at[there], by_y.at[y], y_send, y_recv, y_line(there))

    def own_z():
        return pltpu.make_async_copy(corners.at[2 * lax.div(z, 4) + b], by_z.at[z], z_recv)

    def own_y():
        return pltpu.make_async_copy(folds.at[y], by_y.at[y], y_recv)

    r_half = lax.broadcasted_iota(jnp.int32, (HALF, HALF), 0)
    c_half = lax.broadcasted_iota(jnp.int32, (HALF, HALF), 1)
    on_diag = r_half == c_half
    damp_row = jnp.broadcast_to(jnp.where(x < 2, damp[:, 0:1], damp[:, 1:2]), (1, 128))
    for kk in range(2):
        corners[2 * kk : 2 * kk + 2] = gram[kk, 0].astype(BF16).reshape(2, 8, 16, HALF)
        upper, lower = gram[kk, 1], gram[kk, 2]
        folded = jnp.where(r_half <= c_half, upper, lower).astype(BF16)
        folds[:, kk] = folded.reshape(8, 2, 16, HALF)
        d_up = jnp.sum(jnp.where(on_diag, upper, 0.0), axis=0, keepdims=True)
        d_low = jnp.sum(jnp.where(on_diag, lower, 0.0), axis=0, keepdims=True)
        mine = (expert_at == 4 * parity + 2 * kk + c) & (y == 0) & (zh == 0)
        diag_out[kk, 0:1] = d_up[:, :128]
        diag_out[kk, 1:2] = d_up[:, 128:]
        diag_out[kk, 2:3] = d_low[:, :128]
        diag_out[kk, 3:4] = d_low[:, 128:]
        diag_out[kk, 4:8] = jnp.broadcast_to(jnp.where(mine, damp_row, 0.0), (4, 128))

    def diag_copy():
        return remote(diag_out, diag_y.at[y], diag_send, diag_y_recv, y_line(0))

    @pl.when(y != 0)
    def _():
        diag_copy().start()

    def diag_left():
        @pl.when(y != 0)
        def _():
            diag_copy().wait_send()
    leaving.append(diag_left)

    def z_start(n):
        q = lax.rem(j + n, 4)

        @pl.when(z_there(q) != z)
        def _():
            z_copy(q).start()

    def first_left():
        wait_bytes(folds.at[pl.ds(0, 7)], y_send)

        @pl.when(sums_z)
        def _():
            wait_bytes(corners.at[pl.ds(0, 3)], z_send)

        @pl.when(jnp.logical_not(sums_z))
        def _():
            wait_bytes(corners, z_send)
    leaving.append(first_left)

    for n, ahead in enumerate(((4, 1, 7), (3, 5), (2, 6), ())):
        z_start(n)
        for m in ahead:
            started(y_copy(m))
    own_y().start()

    @pl.when(sums_z)
    def _():
        own_z().start()

    pl.semaphore_wait(both_in, 1)
    tell(cross_in, at_cross)
    tell(cross_in, at_mate)
    wait_bytes(by_y, y_recv)
    sum_y = by_y[0].astype(F32)
    for n in range(1, 8):
        sum_y = sum_y + by_y[n].astype(F32)
    y_sums[...] = sum_y

    def y2_copy(kk, bb):
        return remote(
            y_sums.at[kk, bb], last.at[z], y2_send, last_recv,
            device_at(x, y, 4 * kk + 2 * c + bb, 1),
        )

    def y2_self(kk, bb):
        return (c == 1) & (z == 4 * kk + 2 * c + bb)

    for far in range(2):
        kk = (1 - lax.div(z, 4)) if far == 0 else lax.div(z, 4)
        for bb in range(2):
            @pl.when(jnp.logical_not(y2_self(kk, bb)))
            def _():
                y2_copy(kk, bb).start()

            @pl.when(y2_self(kk, bb))
            def _():
                pltpu.make_async_copy(y_sums.at[kk, bb], last.at[z], last_recv).start()

    def y2_left():
        @pl.when((c == 1) & sums_z)
        def _():
            wait_bytes(last.at[pl.ds(0, 3)], y2_send)

        @pl.when(jnp.logical_not((c == 1) & sums_z))
        def _():
            wait_bytes(last.at[pl.ds(0, 4)], y2_send)
    leaving.append(y2_left)

    def z2_copy(there):
        return remote(
            z_sums.at[there], last.at[y], z2_send, last_recv,
            device_at(x, there, z, 0),
        )

    def z2_self(there):
        return (c == 0) & (there == y)

    @pl.when(sums_z)
    def _():
        wait_bytes(by_z, z_recv)
        sum_z = by_z[0].astype(F32)
        for n in range(1, 8):
            sum_z = sum_z + by_z[n].astype(F32)
        z_sums[...] = sum_z

        for n in (4, 3, 5, 2, 6, 1, 7, 0):
            there = lax.rem(y + n, 8)

            @pl.when(jnp.logical_not(z2_self(there)))
            def _():
                z2_copy(there).start()

            @pl.when(z2_self(there))
            def _():
                pltpu.make_async_copy(z_sums.at[there], last.at[y], last_recv).start()

    def diag_mid_copy(kk):
        return remote(
            diag_mid.at[kk], diag_parts.at[z], diag_mid_send.at[kk], diag_recv,
            device_at(x, 0, 4 * kk + 2 * c, 1),
        )

    def diag_self(kk):
        return (c == 1) & (z == 4 * kk + 2)

    def when_line(step):
        for kk in range(2):
            @pl.when(jnp.logical_not(diag_self(kk)))
            def _():
                step(kk)

    @pl.when(y == 0)
    def _():
        arrived = diag_y.at[pl.ds(1, 7)]
        pltpu.make_async_copy(arrived, arrived, diag_y_recv).wait()
        diag_sum = diag_out[...]
        for n in range(1, 8):
            diag_sum = diag_sum + diag_y[n]
        diag_mid[...] = diag_sum
        when_line(lambda kk: diag_mid_copy(kk).start())
        for kk in range(2):
            @pl.when(diag_self(kk))
            def _():
                pltpu.make_async_copy(diag_mid.at[kk], diag_parts.at[z], diag_recv).start()

    def diag_mid_left():
        @pl.when(y == 0)
        def _():
            when_line(lambda kk: diag_mid_copy(kk).wait_send())
    leaving.append(diag_mid_left)

    def z2_left():
        @pl.when(sums_z & (c == 0))
        def _():
            wait_bytes(z_sums.at[pl.ds(0, 7)], z2_send)

        @pl.when(sums_z & (c == 1))
        def _():
            wait_bytes(z_sums, z2_send)
    leaving.append(z2_left)

    wait_bytes(last, last_recv)
    summed = last[0]
    for n in range(1, 8):
        summed = summed + last[n]
    total[c, row_me] = summed

    def block_line(n, across):
        there = lax.rem(y + n, 8)
        return {"expert": expert_at + across * (2 - 4 * b), "dp": x * 16 + there * 2 + zh}

    def share_copy(n, across):
        own = total.at[c, row_me]
        return remote(own, own, share_send, share_recv.at[b], block_line(n, across))

    def share_on(g):
        group = total.at[c, pl.ds(8 * g, 8)]
        return remote(group, group, on_send.at[g], on_recv.at[g], sibling)

    def diag_to(where):
        return remote(diag_total, diag_total, diag_back_send, diag_back_recv, where)

    pl.semaphore_wait(cross_in, 2)
    tell(mate_in, at_mate)
    block = [(n, across) for n in (4, 3, 5, 2, 6, 1, 7) for across in (1, 0)] + [(0, 1)]
    for n, across in block:
        share_copy(n, across).start()

    @pl.when(sums_diag)
    def _():
        wait_bytes(diag_parts, diag_recv)
        diag_total[...] = jnp.sum(diag_parts[...], axis=0)
        for n, across in block:
            diag_to(block_line(n, across)).start()

    @pl.when(jnp.logical_not(sums_diag))
    def _():
        wait_bytes(diag_total, diag_back_recv)

    @pl.when(c == 1)
    def _():
        diag_to(sibling).start()

    wait_bytes(total.at[c, pl.ds(0, 7)], share_recv.at[b])
    share_on(b).start()
    wait_bytes(total.at[c, pl.ds(0, 8)], share_recv.at[1 - b])
    share_on(1 - b).start()
    for g in range(2):
        group = total.at[sib, pl.ds(8 * g, 8)]
        wait_bytes(group, on_recv.at[g])

    def share_left():
        wait_bytes(total.at[0, pl.ds(0, 15)], share_send)
        for g in range(2):
            share_on(g).wait_send()

        @pl.when(sums_diag)
        def _():
            wait_bytes(diag_y, diag_back_send)

        @pl.when((c == 1) & jnp.logical_not(sums_diag))
        def _():
            wait_bytes(diag_total, diag_back_send)
    leaving.append(share_left)

    corner = total[0].reshape(HALF, HALF) * LOAD_INVERSE
    folded = jnp.concatenate([total[1, 8 * (n % 2) + n // 2] for n in range(16)], axis=0) * LOAD_INVERSE
    turned = jnp.transpose(folded)
    damping = diag_total[4:5, :]
    d_up = jnp.concatenate(
        [diag_total[0:1] * LOAD_INVERSE + damping, diag_total[1:2] * LOAD_INVERSE + damping], axis=1
    )
    d_low = jnp.concatenate(
        [diag_total[2:3] * LOAD_INVERSE + damping, diag_total[3:4] * LOAD_INVERSE + damping], axis=1
    )
    upper = jnp.where(r_half < c_half, folded, jnp.where(r_half > c_half, turned, d_up))
    lower = jnp.where(r_half > c_half, folded, jnp.where(r_half < c_half, turned, d_low))
    corner_turned = jnp.transpose(corner)
    sums_left = jnp.sum(jnp.abs(upper) + jnp.abs(corner_turned), axis=0, keepdims=True)
    sums_right = jnp.sum(jnp.abs(corner) + jnp.abs(lower), axis=0, keepdims=True)
    largest = jnp.max(jnp.maximum(sums_left, sums_right), axis=1, keepdims=True)
    scale = 1.0 / largest
    one = jnp.where(r_half == c_half, 1.0, 0.0)
    for block, at in (
        (one - scale * upper, (slice(0, HALF), slice(0, HALF))),
        (-scale * corner, (slice(0, HALF), slice(HALF, BLOCK))),
        (-scale * corner_turned, (slice(HALF, BLOCK), slice(0, HALF))),
        (one - scale * lower, (slice(HALF, BLOCK), slice(HALF, BLOCK))),
    ):
        top = block.astype(BF16)
        high[at] = top
        low[at] = (block - top.astype(F32)).astype(BF16)

    row_at = lax.broadcasted_iota(jnp.int32, (16, BLOCK), 0)
    col_at = lax.broadcasted_iota(jnp.int32, (16, BLOCK), 1)
    wanted = 8 * (16 * (2 * c + lax.div(row_at, 8)) + 2 * y + b) + lax.rem(row_at, 8)
    unit = jnp.where(col_at == wanted, 1.0, 0.0)
    here = []
    for i in range(2):
        rows = pl.ds(pl.multiple_of(16 * (8 * (2 * c + i) + y), 16), 16)
        both = high[rows, :].astype(F32) + low[rows, :].astype(F32)
        here.append(jnp.where(b == 0, both[:8], both[8:]))
    lead = unit + jnp.concatenate(here, axis=0)
    for _ in range(6):
        lead = unit + split_dot(lead, high[...], low[...])
    result = lead * scale
    rows_out[0] = result[:8]
    rows_out[1] = result[8:]

    pl.semaphore_wait(mate_in, 1)
    e_me = 4 * parity + j

    def out_copy(n):
        i, zt = n // 4, 4 * b + n % 4
        return remote(
            rows_out.at[i], out.at[half_x, e_me], out_send, out_recv, device_at(2 * c + i, y, zt, half_x)
        )

    def out_here(n):
        return (2 * c + n // 4 == x) & (4 * b + n % 4 == z) & (half_x == c)

    for n in range(8):
        @pl.when(jnp.logical_not(out_here(n)))
        def _():
            out_copy(n).start()

        @pl.when(out_here(n))
        def _():
            pltpu.make_async_copy(rows_out.at[n // 4], out.at[half_x, e_me], out_recv).start()

    wait_bytes(out.at[c], out_recv)
    out_on = remote(out.at[c], out.at[c], out_on_send, out_on_recv, sibling)
    out_on.start()
    wait_bytes(out.at[sib], out_on_recv)

    def out_left():
        @pl.when(out_self)
        def _():
            wait_bytes(out.at[0, pl.ds(0, 7)], out_send)

        @pl.when(jnp.logical_not(out_self))
        def _():
            wait_bytes(out.at[0], out_send)
        out_on.wait_send()
    leaving.append(out_left)

    for left in leaving:
        left()


def on_device(features, gradients, route_ids, gate_share, token_mask, damping):
    route = route_ids.T
    share = gate_share.reshape(1, TOKENS_HERE)
    mask = token_mask.reshape(1, TOKENS_HERE)
    damp = damping.reshape(1, 2)
    dma = pltpu.SemaphoreType.DMA
    out = pl.pallas_call(
        refresh,
        out_shape=jax.ShapeDtypeStruct((2, 8, 8, BLOCK), F32),
        in_specs=[pl.BlockSpec(memory_space=pltpu.HBM)] * 6,
        out_specs=pl.BlockSpec(memory_space=pltpu.VMEM),
        scratch_shapes=[
            pltpu.VMEM((2, TOKENS_HERE), jnp.int32),
            pltpu.VMEM((1, TOKENS_HERE), F32),
            pltpu.VMEM((1, TOKENS_HERE), jnp.int32),
            pltpu.VMEM((1, 2), F32),
            pltpu.VMEM((8, TOKENS_HERE, BLOCK), BF16),
            pltpu.VMEM((8, 8, TOKENS_HERE), F32),
            pltpu.VMEM((TOKENS_HERE, BLOCK), BF16),
            pltpu.VMEM((8, TOKENS_HERE), F32),
            pltpu.VMEM((2, 2 * TOKENS_HERE, BLOCK), BF16),
            pltpu.VMEM((2, 3, HALF, HALF), F32),
            pltpu.VMEM((4, 8, 16, HALF), BF16),
            pltpu.VMEM((8, 2, 2, 16, HALF), BF16),
            pltpu.VMEM((2, 8, 128), F32),
            pltpu.VMEM((8, 8, 16, HALF), BF16),
            pltpu.VMEM((8, 2, 2, 16, HALF), BF16),
            pltpu.VMEM((8, 16, HALF), F32),
            pltpu.VMEM((2, 2, 16, HALF), F32),
            pltpu.VMEM((8, 16, HALF), F32),
            pltpu.VMEM((8, 2, 8, 128), F32),
            pltpu.VMEM((2, 8, 128), F32),
            pltpu.VMEM((8, 8, 128), F32),
            pltpu.VMEM((2, 16, 16, HALF), F32),
            pltpu.VMEM((8, 128), F32),
            pltpu.VMEM((BLOCK, BLOCK), BF16),
            pltpu.VMEM((BLOCK, BLOCK), BF16),
            pltpu.VMEM((2, 8, BLOCK), F32),
            dma((6,)), dma, dma((3, PARTS)), dma((4,)), dma, dma((7,)),
            *[pltpu.SemaphoreType.REGULAR] * 5,
            dma, dma, dma, dma, dma, dma, dma,
            dma, dma, dma((2,)), dma, dma, dma,
            dma, dma((2,)), dma((2,)), dma((2,)), dma, dma, dma, dma,
        ],
        compiler_params=pltpu.CompilerParams(
            collective_id=0, has_side_effects=True, vmem_limit_bytes=40 * 1024 * 1024
        ),
    )(*[pltpu.with_memory_space_constraint(a, pltpu.HBM) for a in (features, gradients, route, share, mask, damp)])
    return out[0].reshape(8, 1, 8, BLOCK), out[1].reshape(8, 1, 8, BLOCK)


def solution(mesh):
    placed = (
        P(("expert", "dp"), None),
        P(("expert", "dp"), None),
        P(("expert", "dp"), None),
        P(("expert", "dp")),
        P(("expert", "dp")),
        P("expert", None, None),
    )
    return jax.shard_map(
        on_device,
        mesh=mesh,
        in_specs=placed,
        out_specs=(P(None, None, "dp", None), P(None, None, "dp", None)),
        check_vma=False,
    )
```
